32 devices in a mesh: row: 8 (over z, x), col: 4 (over y, core).
Axes of the slice: x: 2, y: 2, z: 4, core: 2. Of those that a mesh axis runs over, the one named last changes fastest.
Arguments:
- panel_block: float32 [16384, 128], P('row'), may hold values from -8 to 8, as said below
- trailing: float32 [16384, 16384], P('row', 'col'), may hold values from -80 to 80
Outputs:
- reduced: float32 [16384, 16384], P('row', 'col')
- band_block: float32 [128, 128], replicated
- first_factor: float32 [128, 128], replicated
The draws below stay inside these ranges and needn't reach their ends.
Inputs may be any that keep to these rules, and one draw needn't show every extreme that they name: `panel_block`: entries of order the inverse square root of 16384; rows may differ in scale; the columns may be nearly dependent, with a condition number of the panel up to a few thousand; the first 128 rows of the orthonormal basis have spectral norm at most 0.8, so that I + top^T needs no pivoting.
All inputs are finite; a program needn't handle non-finite values.
Results may differ from the reference program's by a relative error of at most 0.0017.
Values sent between devices are 32-bit elements; how exact they have to be, the bound alone decides.
No kernel may reach another device: no remote copies, remote signals or barrier semaphores. Data moves between devices by JAX's collectives and lax.ppermute only.
A program may use at most 128 MiB of HBM per device.

```python
import math
import jax
import jax.numpy as jnp
from jax import lax

N = 16384
B = 128


def draw_panel_block(key, part):
    first_key = jax.random.fold_in(jax.random.fold_in(key, 11), 0)
    second_key = jax.random.fold_in(jax.random.fold_in(key, 11), 1)
    fourth_key = jax.random.fold_in(jax.random.fold_in(key, 11), 3)
    common = jnp.clip(jax.random.normal(first_key, (N, 1), jnp.float32), -6.0, 6.0)
    own_part = jnp.clip(jax.random.normal(second_key, (N, B), jnp.float32), -6.0, 6.0)
    half_width = B // 2
    steps_down = jnp.minimum(jnp.arange(B, dtype=jnp.float32), float(half_width - 1))
    grade = jnp.exp(steps_down * (math.log(0.006) / (half_width - 1)))
    order = jax.random.permutation(fourth_key, B)
    grade = grade[order]
    values = (common + own_part * grade[None, :]) / jnp.sqrt(1.0 + grade * grade)[None, :]
    rising = jnp.exp(jnp.arange(N, dtype=jnp.float32) * (math.log(3.0) / N))[:, None]
    leading = jnp.where(jnp.arange(N) < B, 12.0, 1.0).astype(jnp.float32)[:, None]
    values = values * rising * leading
    return jnp.clip(values * float(N) ** (-0.5), -8.0, 8.0)


def draw_trailing(key, part):
    first_key = jax.random.fold_in(jax.random.fold_in(key, 23), 0)
    base = jnp.clip(jax.random.normal(first_key, (N, N), jnp.float32), -6.0, 6.0)
    values = (base + base.T) * 0.7071
    return jnp.clip(values, -80.0, 80.0)


def setup_inputs(seed: int = 0) -> dict:
    streams_of = jax.random.split(jax.random.key(seed), 3)
    panel_block = draw_panel_block(jax.random.fold_in(streams_of[2], 71), 0)
    trailing = draw_trailing(jax.random.fold_in(streams_of[2], 71), 0)
    return {"panel_block": panel_block, "trailing": trailing}


HIGH = lax.Precision.HIGHEST

def gram_of(values):
    return jnp.dot(values.T, values, precision=HIGH, preferred_element_type=values.dtype)

def invert_square(square):
    size_n = square.shape[0]
    augmented = jnp.concatenate([square, jnp.eye(size_n, dtype=square.dtype)], axis=1)
    positions = jnp.arange(size_n)

    def eliminate(pivot, current):
        pivot_row = lax.dynamic_index_in_dim(current, pivot, 0, keepdims=False)
        pivot_row = pivot_row / pivot_row[pivot]
        column = lax.dynamic_index_in_dim(current, pivot, 1, keepdims=False)
        column = column - (positions == pivot).astype(current.dtype)
        return current - column[:, None] * pivot_row[None, :]
    augmented = lax.fori_loop(0, size_n, eliminate, augmented)
    return augmented[:, size_n:]

def right_solve(factor, values):
    return lax.linalg.triangular_solve(factor, values, left_side=False, lower=True, transpose_a=True)

def reference(panel_block, trailing):
    first_factor = jnp.linalg.cholesky(gram_of(panel_block))
    first_basis = right_solve(first_factor, panel_block)
    second_factor = jnp.linalg.cholesky(gram_of(first_basis))
    basis = right_solve(second_factor, first_basis)
    band_block = -jnp.dot(second_factor.T, first_factor.T, precision=HIGH)
    width = basis.shape[1]
    kernel = invert_square(jnp.eye(width, dtype=basis.dtype) + basis[:width].T)
    ident = (jnp.arange(basis.shape[0])[:, None] == jnp.arange(width)[None, :]).astype(basis.dtype)
    vectors = basis + ident
    applied = jnp.dot(jnp.dot(trailing, vectors, precision=HIGH), kernel, precision=HIGH)
    inner = jnp.dot(kernel.T, jnp.dot(vectors.T, applied, precision=HIGH), precision=HIGH)
    update = applied - 0.5 * jnp.dot(vectors, inner, precision=HIGH)
    reduced = trailing - jnp.dot(vectors, update.T, precision=HIGH) - jnp.dot(update, vectors.T, precision=HIGH)
    return (reduced, band_block, first_factor)
```

```python
import functools

import jax
import jax.numpy as jnp
from jax import lax
from jax.experimental import pallas as pl
from jax.experimental.pallas import tpu as pltpu
from jax.sharding import PartitionSpec as P

HIGH = lax.Precision.HIGHEST
F32 = jnp.float32
BF16 = jnp.bfloat16
SUB = 8


def dot_nn(a, b):
    return lax.dot_general(a, b, (((1,), (0,)), ((), ())), precision=HIGH, preferred_element_type=F32)


def dot_nt(a, b):
    return lax.dot_general(a, b, (((1,), (1,)), ((), ())), precision=HIGH, preferred_element_type=F32)


def dot_tn(a, b):
    return lax.dot_general(a, b, (((0,), (0,)), ((), ())), precision=HIGH, preferred_element_type=F32)


def dot_fast(a, b):
    return lax.dot_general(a, b, (((1,), (0,)), ((), ())), preferred_element_type=F32)


def lane_copy(tile, lane):
    return jnp.broadcast_to(tile[:, lane : lane + 1], tile.shape)


def row_copy(tile, row):
    return jnp.broadcast_to(tile[row : row + 1, :], tile.shape)


def cholesky_tiles(tiles):
    size = tiles[0].shape[1]
    count = len(tiles)
    tiles = list(tiles)
    lanes = lax.broadcasted_iota(jnp.int32, (SUB, size), 1)
    subs = lax.broadcasted_iota(jnp.int32, (SUB, size), 0)
    upper, inverse = [], []
    for block in range(count):
        base = block * SUB
        here = (lanes >= base) & (lanes < base + SUB)
        columns = [[lane_copy(tiles[i], base + k) for k in range(SUB)] for i in range(block, count)]
        right = jnp.where(lanes >= base, tiles[block], 0.0)
        left = jnp.where(lanes < base, tiles[block], 0.0)
        left = jnp.where(lanes - base == subs, 1.0, left)
        out_upper, out_inverse = jnp.zeros_like(right), jnp.zeros_like(left)
        below = [jnp.where(here, 0.0, tiles[i]) for i in range(block + 1, count)]
        for k in range(SUB):
            diag = columns[0]
            pivot = row_copy(diag[k], k)
            root = lax.rsqrt(pivot)
            recip = 1.0 / pivot
            right_row, left_row = row_copy(right, k), row_copy(left, k)
            out_upper = jnp.where(subs == k, right_row * root, out_upper)
            out_inverse = jnp.where(subs == k, left_row * root, out_inverse)
            packed = jnp.where(lanes < base + SUB, left_row, right_row) * recip
            rows = {l: row_copy(diag[l], k) * recip for l in range(k + 1, SUB)}
            factor = jnp.where(subs > k, diag[k], 0.0)
            right = right - factor * (right_row * recip)
            left = left - factor * (left_row * recip)
            for i in range(count - block):
                for l in range(k + 1, SUB):
                    if i == 0:
                        columns[0][l] = columns[0][l] - factor * rows[l]
                    else:
                        columns[i][l] = columns[i][l] - columns[i][k] * rows[l]
                if i:
                    below[i - 1] = below[i - 1] - columns[i][k] * packed
        for i in range(block + 1, count):
            tiles[i] = below[i - block - 1]
        upper.append(jnp.where(lanes >= base + subs, out_upper, 0.0))
        inverse.append(out_inverse)
    return upper, inverse


def invert_tiles(tiles):
    size = tiles[0].shape[1]
    count = len(tiles)
    tiles = list(tiles)
    lanes = lax.broadcasted_iota(jnp.int32, (SUB, size), 1)
    subs = lax.broadcasted_iota(jnp.int32, (SUB, size), 0)
    for block in range(count):
        base = block * SUB
        here = (lanes >= base) & (lanes < base + SUB)
        columns = [[lane_copy(tiles[i], base + k) for k in range(SUB)] for i in range(count)]
        diag = list(columns[block])
        row = jnp.where(here, jnp.where(lanes - base == subs, 1.0, 0.0), tiles[block])
        for k in range(SUB):
            recip = 1.0 / row_copy(diag[k], k)
            own = subs == k
            pivot_row = row_copy(row, k) * recip
            rows = {l: row_copy(diag[l], k) * recip for l in range(k + 1, SUB)}
            row = jnp.where(own, pivot_row, row - diag[k] * pivot_row)
            for l in range(k + 1, SUB):
                diag[l] = jnp.where(own, rows[l], diag[l] - diag[k] * rows[l])
        spread = [row_copy(row, k) for k in range(SUB)]
        for i in range(count):
            if i == block:
                continue
            value = jnp.where(here, 0.0, tiles[i])
            for k in range(SUB):
                value = value - columns[i][k] * spread[k]
            tiles[i] = value
        tiles[block] = row
    return tiles


def tiles_of(ref):
    return [ref[i * SUB : (i + 1) * SUB, :] for i in range(ref.shape[0] // SUB)]


def first_kernel(gram_ref, panel_ref, factor_ref, inverse_ref, basis_ref, second_ref):
    upper, inverse = cholesky_tiles(tiles_of(gram_ref))
    factor_ref[...] = jnp.concatenate(upper, axis=0).T
    inverse_ref[...] = jnp.concatenate(inverse, axis=0)
    basis_ref[...] = dot_nt(panel_ref[...], inverse_ref[...])
    basis = basis_ref[...]
    second_ref[...] = dot_tn(basis, basis)


def first_pass(gram, panel):
    square = jax.ShapeDtypeStruct(gram.shape, F32)
    return pl.pallas_call(
        first_kernel,
        out_shape=(square, square, jax.ShapeDtypeStruct(panel.shape, F32), square),
        compiler_params=pltpu.CompilerParams(vmem_limit_bytes=32 * 1024 * 1024),
        name="first_pass",
    )(gram, panel)


def second_kernel(gram_ref, first_ref, top_ref, inverse_ref, band_ref, kernel_ref):
    upper, inverse = cholesky_tiles(tiles_of(gram_ref))
    inverse_ref[...] = jnp.concatenate(inverse, axis=0)
    band_ref[...] = -dot_nt(jnp.concatenate(upper, axis=0), first_ref[...])
    size = gram_ref.shape[0]
    rows = lax.broadcasted_iota(jnp.int32, (size, size), 0)
    lanes = lax.broadcasted_iota(jnp.int32, (size, size), 1)
    eye = jnp.where(rows == lanes, 1.0, 0.0)
    kernel_ref[...] = eye + dot_nt(inverse_ref[...], top_ref[...])
    kernel_ref[...] = jnp.concatenate(invert_tiles(tiles_of(kernel_ref)), axis=0)


def second_pass(gram, first_factor, top):
    square = jax.ShapeDtypeStruct(gram.shape, F32)
    return pl.pallas_call(
        second_kernel,
        out_shape=(square, square, square),
        compiler_params=pltpu.CompilerParams(vmem_limit_bytes=32 * 1024 * 1024),
        name="second_pass",
    )(gram, first_factor, top)


def split(value):
    high = value.astype(BF16)
    return high, (value - high.astype(F32)).astype(BF16)


def product_kernel(low_ref, trailing_ref, vectors_ref, out_ref, both):
    del low_ref
    part = pl.program_id(1)
    width = out_ref.shape[1]

    @pl.when(pl.program_id(0) == 0)
    def _():
        high, low = split(vectors_ref[0])
        both[part, :, :width] = high
        both[part, :, width:] = low

    high, low = split(trailing_ref[...])
    right = both[part]
    value = dot_fast(high, right) + dot_fast(low, right)
    value = value[:, :width] + value[:, width:]

    @pl.when(part == 0)
    def _():
        out_ref[...] = value

    @pl.when(part > 0)
    def _():
        out_ref[...] += value


def product(low, trailing, vectors):
    rows = trailing.shape[0]
    ratio, depth, width = vectors.shape
    tile = min(rows, 512)
    return pl.pallas_call(
        product_kernel,
        out_shape=jax.ShapeDtypeStruct((rows, width), F32),
        grid_spec=pltpu.PrefetchScalarGridSpec(
            num_scalar_prefetch=1,
            grid=(rows // tile, ratio),
            in_specs=[
                pl.BlockSpec((tile, depth), lambda i, t, low: (i, t ^ low[0])),
                pl.BlockSpec((1, depth, width), lambda i, t, low: (t, 0, 0)),
            ],
            out_specs=pl.BlockSpec((tile, width), lambda i, t, low: (i, 0)),
            scratch_shapes=[pltpu.VMEM((ratio, depth, 2 * width), BF16)],
        ),
        compiler_params=pltpu.CompilerParams(vmem_limit_bytes=48 * 1024 * 1024),
        name="product",
    )(low, trailing, vectors)


def update_kernel(low_ref, trailing_ref, left_ref, applied_ref, vectors_ref, out_ref, high_ref, rest_ref):
    del low_ref
    width = vectors_ref.shape[2]

    @pl.when(pl.program_id(1) == 0)
    def _():
        for place, ref in ((0, applied_ref), (width, vectors_ref)):
            high, rest = split(ref[0].T)
            high_ref[place : place + width, :] = high
            rest_ref[place : place + width, :] = rest

    high, rest = split(left_ref[...])
    value = dot_fast(high, high_ref[...]) + dot_fast(high, rest_ref[...]) + dot_fast(rest, high_ref[...])
    out_ref[...] = trailing_ref[...] - value


def update(low, trailing, left, applied, vectors):
    rows = trailing.shape[0]
    ratio, depth, width = vectors.shape
    tile = min(rows, 512)
    return pl.pallas_call(
        update_kernel,
        out_shape=jax.ShapeDtypeStruct(trailing.shape, F32),
        grid_spec=pltpu.PrefetchScalarGridSpec(
            num_scalar_prefetch=1,
            grid=(ratio, rows // tile),
            in_specs=[
                pl.BlockSpec((tile, depth), lambda t, i, low: (i, t ^ low[0])),
                pl.BlockSpec((tile, 2 * width), lambda t, i, low: (i, 0)),
                pl.BlockSpec((1, depth, width), lambda t, i, low: (t, 0, 0)),
                pl.BlockSpec((1, depth, width), lambda t, i, low: (t, 0, 0)),
            ],
            out_specs=pl.BlockSpec((tile, depth), lambda t, i, low: (i, t ^ low[0])),
            scratch_shapes=[pltpu.VMEM((2 * width, depth), BF16)] * 2,
        ),
        compiler_params=pltpu.CompilerParams(vmem_limit_bytes=48 * 1024 * 1024),
        name="update",
    )(low, trailing, left, applied, vectors)


def swap(value, axis, bit):
    count = lax.axis_size(axis)
    return lax.ppermute(value, axis, [(i, i ^ bit) for i in range(count)])


def bits_of(count):
    return [1 << b for b in range(count.bit_length() - 1)]


def sum_small(value, axis):
    for bit in bits_of(lax.axis_size(axis)):
        value = value + swap(value, axis, bit)
    return value


def sum_over_col(value):
    half = value.shape[0] // 2
    first, *others = bits_of(lax.axis_size("col"))
    mine = lax.axis_index("col") & 1
    keep = lax.dynamic_slice_in_dim(value, mine * half, half, 0)
    give = lax.dynamic_slice_in_dim(value, (1 - mine) * half, half, 0)
    keep = keep + swap(give, "col", first)
    for bit in others:
        keep = keep + swap(keep, "col", bit)
    other = swap(keep, "col", first)
    return jnp.where(mine == 0, jnp.concatenate([keep, other]), jnp.concatenate([other, keep]))


def gather_column_block(value):
    row_n, col_n = lax.axis_size("row"), lax.axis_size("col")
    ratio = row_n // col_n
    row, col = lax.axis_index("row"), lax.axis_index("col")
    done = 0
    away = (row // ratio) ^ col
    for bit in reversed(bits_of(col_n)):
        pairs = []
        for r in range(row_n):
            for c in range(col_n):
                if ((r // ratio) ^ c) & ~done == 0:
                    pairs.append((r * col_n + c, (r ^ (bit * ratio)) * col_n + c))
        moved = lax.ppermute(value, ("row", "col"), pairs)
        value = jnp.where((away & ~done) == bit, moved, value)
        done |= bit
    blocks = value[None]
    for bit in bits_of(ratio):
        blocks = jnp.concatenate([blocks, swap(blocks, "row", bit)])
    return blocks


def broadcast_col(value):
    col_n = lax.axis_size("col")
    col = lax.axis_index("col")
    for bit in bits_of(col_n):
        moved = lax.ppermute(value, "col", [(i, i + bit) for i in range(bit)])
        value = jnp.where((col >= bit) & (col < 2 * bit), moved, value)
    return value


def body(panel_block, trailing):
    shard_rows, width = panel_block.shape
    row, col = lax.axis_index("row"), lax.axis_index("col")
    ratio = lax.axis_size("row") // lax.axis_size("col")
    low = row % ratio
    low_arg = low.astype(jnp.int32)[None]

    first_gram = sum_small(dot_tn(panel_block, panel_block), "row")
    panel_blocks = gather_column_block(panel_block)
    top_panel = broadcast_col(
        lax.dynamic_index_in_dim(panel_blocks, low, 0, keepdims=False)[:width]
    )
    first_factor, first_inverse, first_basis, second_part = first_pass(first_gram, panel_block)
    second_gram = sum_small(second_part, "row")
    first_blocks = dot_nt(panel_blocks.reshape(-1, width), first_inverse)
    first_top = dot_nt(top_panel, first_inverse)
    raw = product(low_arg, trailing, first_blocks.reshape(ratio, shard_rows, width))

    second_inverse, band_block, kernel = second_pass(second_gram, first_factor, first_top)

    lane = jnp.arange(width)
    own_rows = row * shard_rows + jnp.arange(shard_rows)
    vectors = dot_nt(first_basis, second_inverse) + (own_rows[:, None] == lane).astype(F32)
    sub = jnp.arange(ratio) ^ low
    block_rows = (col * ratio + sub)[:, None] * shard_rows + jnp.arange(shard_rows)
    block_vectors = dot_nt(first_blocks, second_inverse).reshape(ratio, shard_rows, width)
    block_vectors = block_vectors + (block_rows[:, :, None] == lane).astype(F32)

    part = dot_nt(raw, second_inverse) + jnp.where(col == 0, trailing[:, :width], 0.0)
    own = sum_over_col(part)
    blocks = gather_column_block(own)
    inner = sum_small(dot_tn(vectors, own), "row")
    inner = dot_tn(kernel, dot_nn(inner, kernel))
    left = jnp.concatenate(
        [dot_nt(vectors, kernel), dot_nn(own, kernel) - dot_nn(vectors, inner)], axis=1
    )
    reduced = update(low_arg, trailing, left, blocks, block_vectors)
    return (reduced, band_block, first_factor)


def solution(mesh):
    in_specs = (P("row", None), P("row", "col"))
    out_specs = (P("row", "col"), P(), P())
    return jax.shard_map(body, mesh=mesh, in_specs=in_specs, out_specs=out_specs, check_vma=False)
```

```python
import functools

import jax
import jax.numpy as jnp
from jax import lax
from jax.experimental import pallas as pl
from jax.experimental.pallas import tpu as pltpu
from jax.sharding import PartitionSpec as P

HIGH = lax.Precision.HIGHEST
F32 = jnp.float32
BF16 = jnp.bfloat16
SUB = 8


def dot_nn(a, b):
    return lax.dot_general(a, b, (((1,), (0,)), ((), ())), precision=HIGH, preferred_element_type=F32)


def dot_nt(a, b):
    return lax.dot_general(a, b, (((1,), (1,)), ((), ())), precision=HIGH, preferred_element_type=F32)


def dot_tn(a, b):
    return lax.dot_general(a, b, (((0,), (0,)), ((), ())), precision=HIGH, preferred_element_type=F32)


def dot_fast(a, b):
    return lax.dot_general(a, b, (((1,), (0,)), ((), ())), preferred_element_type=F32)


def lane_copy(tile, lane):
    return jnp.broadcast_to(tile[:, lane : lane + 1], tile.shape)


def row_copy(tile, row):
    return jnp.broadcast_to(tile[row : row + 1, :], tile.shape)


def cholesky_tiles(tiles):
    size = tiles[0].shape[1]
    count = len(tiles)
    tiles = list(tiles)
    lanes = lax.broadcasted_iota(jnp.int32, (SUB, size), 1)
    subs = lax.broadcasted_iota(jnp.int32, (SUB, size), 0)
    upper, inverse = [], []
    for block in range(count):
        base = block * SUB
        here = (lanes >= base) & (lanes < base + SUB)
        columns = [[lane_copy(tiles[i], base + k) for k in range(SUB)] for i in range(block, count)]
        right = jnp.where(lanes >= base, tiles[block], 0.0)
        left = jnp.where(lanes < base, tiles[block], 0.0)
        left = jnp.where(lanes - base == subs, 1.0, left)
        out_upper, out_inverse = jnp.zeros_like(right), jnp.zeros_like(left)
        below = [jnp.where(here, 0.0, tiles[i]) for i in range(block + 1, count)]
        for k in range(SUB):
            diag = columns[0]
            pivot = row_copy(diag[k], k)
            root = lax.rsqrt(pivot)
            recip = 1.0 / pivot
            right_row, left_row = row_copy(right, k), row_copy(left, k)
            out_upper = jnp.where(subs == k, right_row * root, out_upper)
            out_inverse = jnp.where(subs == k, left_row * root, out_inverse)
            packed = jnp.where(lanes < base + SUB, left_row, right_row) * recip
            rows = {l: row_copy(diag[l], k) * recip for l in range(k + 1, SUB)}
            factor = jnp.where(subs > k, diag[k], 0.0)
            right = right - factor * (right_row * recip)
            left = left - factor * (left_row * recip)
            for i in range(count - block):
                for l in range(k + 1, SUB):
                    if i == 0:
                        columns[0][l] = columns[0][l] - factor * rows[l]
                    else:
                        columns[i][l] = columns[i][l] - columns[i][k] * rows[l]
                if i:
                    below[i - 1] = below[i - 1] - columns[i][k] * packed
        for i in range(block + 1, count):
            tiles[i] = below[i - block - 1]
        upper.append(jnp.where(lanes >= base + subs, out_upper, 0.0))
        inverse.append(out_inverse)
    return upper, inverse


def invert_tiles(tiles):
    size = tiles[0].shape[1]
    count = len(tiles)
    tiles = list(tiles)
    lanes = lax.broadcasted_iota(jnp.int32, (SUB, size), 1)
    subs = lax.broadcasted_iota(jnp.int32, (SUB, size), 0)
    for block in range(count):
        base = block * SUB
        here = (lanes >= base) & (lanes < base + SUB)
        columns = [[lane_copy(tiles[i], base + k) for k in range(SUB)] for i in range(count)]
        diag = list(columns[block])
        row = jnp.where(here, jnp.where(lanes - base == subs, 1.0, 0.0), tiles[block])
        for k in range(SUB):
            recip = 1.0 / row_copy(diag[k], k)
            own = subs == k
            pivot_row = row_copy(row, k) * recip
            rows = {l: row_copy(diag[l], k) * recip for l in range(k + 1, SUB)}
            row = jnp.where(own, pivot_row, row - diag[k] * pivot_row)
            for l in range(k + 1, SUB):
                diag[l] = jnp.where(own, rows[l], diag[l] - diag[k] * rows[l])
        spread = [row_copy(row, k) for k in range(SUB)]
        for i in range(count):
            if i == block:
                continue
            value = jnp.where(here, 0.0, tiles[i])
            for k in range(SUB):
                value = value - columns[i][k] * spread[k]
            tiles[i] = value
        tiles[block] = row
    return tiles


def tiles_of(ref):
    return [ref[i * SUB : (i + 1) * SUB, :] for i in range(ref.shape[0] // SUB)]


def first_kernel(gram_ref, panel_ref, factor_ref, inverse_ref, basis_ref, second_ref):
    upper, inverse = cholesky_tiles(tiles_of(gram_ref))
    factor_ref[...] = jnp.concatenate(upper, axis=0).T
    inverse_ref[...] = jnp.concatenate(inverse, axis=0)
    basis_ref[...] = dot_nt(panel_ref[...], inverse_ref[...])
    basis = basis_ref[...]
    second_ref[...] = dot_tn(basis, basis)


def first_pass(gram, panel):
    square = jax.ShapeDtypeStruct(gram.shape, F32)
    return pl.pallas_call(
        first_kernel,
        out_shape=(square, square, jax.ShapeDtypeStruct(panel.shape, F32), square),
        compiler_params=pltpu.CompilerParams(vmem_limit_bytes=32 * 1024 * 1024),
        name="first_pass",
    )(gram, panel)


def second_kernel(gram_ref, upper_ref, inverse_ref):
    upper, inverse = cholesky_tiles(tiles_of(gram_ref))
    upper_ref[...] = jnp.concatenate(upper, axis=0)
    inverse_ref[...] = jnp.concatenate(inverse, axis=0)


def second_pass(gram):
    square = jax.ShapeDtypeStruct(gram.shape, F32)
    return pl.pallas_call(second_kernel, out_shape=(square, square), name="second_pass")(gram)


def small_kernel(upper_ref, inverse_ref, first_ref, top_ref, band_ref, kernel_ref):
    band_ref[...] = -dot_nt(upper_ref[...], first_ref[...])
    size = upper_ref.shape[0]
    rows = lax.broadcasted_iota(jnp.int32, (size, size), 0)
    lanes = lax.broadcasted_iota(jnp.int32, (size, size), 1)
    eye = jnp.where(rows == lanes, 1.0, 0.0)
    kernel_ref[...] = eye + dot_nt(inverse_ref[...], top_ref[...])
    kernel_ref[...] = jnp.concatenate(invert_tiles(tiles_of(kernel_ref)), axis=0)


def small_pass(upper, inverse, first_factor, top):
    square = jax.ShapeDtypeStruct(upper.shape, F32)
    return pl.pallas_call(small_kernel, out_shape=(square, square), name="small_pass")(
        upper, inverse, first_factor, top
    )


def split(value):
    high = value.astype(BF16)
    return high, (value - high.astype(F32)).astype(BF16)


def fetch(away, holder, others, into, sem):
    @pl.when(away == 0)
    def _():
        copy = pltpu.make_async_copy(holder, into, sem)
        copy.start()
        copy.wait()

    @pl.when(away != 0)
    def _():
        place = 0
        for other in others:
            count = other.shape[0]
            copy = pltpu.make_async_copy(other, into.at[pl.ds(place, count)], sem)
            copy.start()
            copy.wait()
            place += count


def product_kernel(index_ref, trailing_ref, inverse_ref, before_ref, holder_ref, *refs):
    *others, out_ref, basis_ref, panel, both, sem = refs
    width = out_ref.shape[1]

    @pl.when(pl.program_id(0) == 0)
    def _():
        fetch(index_ref[1], holder_ref, others, panel, sem)
        basis_ref[...] = dot_nt(panel[...], inverse_ref[...])
        high, low = split(basis_ref[...])
        both[:, :width] = high
        both[:, width:] = low

    high, low = split(trailing_ref[...])
    right = both[...]
    value = dot_fast(high, right) + dot_fast(low, right)
    out_ref[...] = before_ref[...] + (value[:, :width] + value[:, width:])


def product(index, trailing, inverse, before, holder, others):
    rows = trailing.shape[0]
    depth, width = holder.shape
    tile = min(rows, 512)
    anywhere = pl.BlockSpec(memory_space=pl.ANY)
    return pl.pallas_call(
        product_kernel,
        out_shape=(
            jax.ShapeDtypeStruct((rows, width), F32),
            jax.ShapeDtypeStruct((depth, width), F32),
        ),
        grid_spec=pltpu.PrefetchScalarGridSpec(
            num_scalar_prefetch=1,
            grid=(rows // tile,),
            in_specs=[
                pl.BlockSpec((tile, depth), lambda i, index: (i, index[0])),
                pl.BlockSpec((width, width), lambda i, index: (0, 0)),
                pl.BlockSpec((tile, width), lambda i, index: (i, 0)),
                anywhere,
                *[anywhere for _ in others],
            ],
            out_specs=(
                pl.BlockSpec((tile, width), lambda i, index: (i, 0)),
                pl.BlockSpec((depth, width), lambda i, index: (0, 0)),
            ),
            scratch_shapes=[
                pltpu.VMEM((depth, width), F32),
                pltpu.VMEM((depth, 2 * width), BF16),
                pltpu.SemaphoreType.DMA,
            ],
        ),
        compiler_params=pltpu.CompilerParams(vmem_limit_bytes=48 * 1024 * 1024),
        cost_estimate=pl.CostEstimate(
            flops=8 * rows * depth * width, bytes_accessed=4 * rows * depth, transcendentals=0
        ),
        name="product",
    )(index, trailing, inverse, before, holder, *others)


def update_kernel(index_ref, trailing_ref, left_ref, vectors_ref, holder_ref, *refs):
    *others, _, out_ref, applied, right = refs[:-1]
    sem = refs[-1]
    width = vectors_ref.shape[1]

    @pl.when(pl.program_id(0) == 0)
    def _():
        fetch(index_ref[1], holder_ref, others, applied, sem)
        for place, ref in ((0, applied), (width, vectors_ref)):
            high, low = split(ref[...].T)
            right[place : place + width, :] = high
            right[2 * width + place : 3 * width + place, :] = low
            right[4 * width + place : 5 * width + place, :] = high

    high, low = split(left_ref[...])
    left = jnp.concatenate([high, high, low], axis=1)
    out_ref[...] = trailing_ref[...] - dot_fast(left, right[...])


def update(index, trailing, left, vectors, holder, others, reduced):
    rows = trailing.shape[0]
    depth, width = vectors.shape
    tile = min(rows, 512)
    anywhere = pl.BlockSpec(memory_space=pl.ANY)
    aliases = {}
    if reduced is None:
        reduced = index
    else:
        aliases = {5 + len(others): 0}
    return pl.pallas_call(
        update_kernel,
        out_shape=jax.ShapeDtypeStruct(trailing.shape, F32),
        grid_spec=pltpu.PrefetchScalarGridSpec(
            num_scalar_prefetch=1,
            grid=(rows // tile,),
            in_specs=[
                pl.BlockSpec((tile, depth), lambda i, index: (i, index[0])),
                pl.BlockSpec((tile, 2 * width), lambda i, index: (i, 0)),
                pl.BlockSpec((depth, width), lambda i, index: (0, 0)),
                anywhere,
                *[anywhere for _ in others],
                anywhere,
            ],
            out_specs=pl.BlockSpec((tile, depth), lambda i, index: (i, index[0])),
            scratch_shapes=[
                pltpu.VMEM((depth, width), F32),
                pltpu.VMEM((6 * width, depth), BF16),
                pltpu.SemaphoreType.DMA,
            ],
        ),
        input_output_aliases=aliases,
        compiler_params=pltpu.CompilerParams(vmem_limit_bytes=48 * 1024 * 1024),
        cost_estimate=pl.CostEstimate(
            flops=12 * rows * depth * width, bytes_accessed=8 * rows * depth, transcendentals=0
        ),
        name="update",
    )(index, trailing, left, vectors, holder, *others, reduced)


def applied_kernel(index_ref, raw_ref, inverse_ref, lead_ref, give_ref, keep_ref):
    value = dot_nt(raw_ref[...], inverse_ref[...])
    value = value + jnp.where(index_ref[1] == 0, lead_ref[...], 0.0)

    @pl.when(pl.program_id(0) == 0)
    def _():
        give_ref[...] = value

    @pl.when(pl.program_id(0) == 1)
    def _():
        keep_ref[...] = value


def applied_halves(index, raw, inverse, trailing):
    rows, width = raw.shape
    half = rows // 2
    whole = pl.BlockSpec((half, width), lambda i, index: (0, 0))
    out = jax.ShapeDtypeStruct((half, width), F32)
    return pl.pallas_call(
        applied_kernel,
        out_shape=(out, out),
        grid_spec=pltpu.PrefetchScalarGridSpec(
            num_scalar_prefetch=1,
            grid=(2,),
            in_specs=[
                pl.BlockSpec((half, width), lambda i, index: (1 - (index[0] ^ i), 0)),
                pl.BlockSpec((width, width), lambda i, index: (0, 0)),
                pl.BlockSpec((half, width), lambda i, index: (1 - (index[0] ^ i), 0)),
            ],
            out_specs=(whole, whole),
        ),
        compiler_params=pltpu.CompilerParams(vmem_limit_bytes=32 * 1024 * 1024),
        name="applied",
    )(index, raw, inverse, trailing)


def after(value, *others):
    return lax.optimization_barrier((value, *others))[0]


def swap(value, axis, bit):
    count = lax.axis_size(axis)
    return lax.ppermute(value, axis, [(i, i ^ bit) for i in range(count)])


def bits_of(count):
    return [1 << b for b in range(count.bit_length() - 1)]


def sum_small(value, axis, bits):
    for bit in bits:
        value = value + swap(value, axis, bit)
    return value


class Gather:
    def __init__(self):
        self.row_n, self.col_n = lax.axis_size("row"), lax.axis_size("col")
        self.ratio = self.row_n // self.col_n
        self.away = (lax.axis_index("row") // self.ratio) ^ lax.axis_index("col")

    def move(self, value, holds, to_row):
        pairs = []
        for r in range(self.row_n):
            for c in range(self.col_n):
                if holds((r // self.ratio) ^ c):
                    pairs.append((r * self.col_n + c, to_row(r) * self.col_n + c))
        return lax.ppermute(value, ("row", "col"), pairs)

    def relay(self, value):
        done = 0
        for bit in reversed(bits_of(self.col_n)[1:]):
            moved = self.move(
                value, lambda d: d & ~done == 0, lambda r: r ^ (bit * self.ratio)
            )
            value = jnp.where((self.away & ~done) == bit, moved, value)
            done |= bit
        return value

    def near(self, value):
        holds = lambda d: d & 1 == 0
        return (
            self.move(value, holds, lambda r: r ^ self.ratio),
            self.move(value, holds, lambda r: r ^ 1),
        )

    def across(self, moved_high, moved_low):
        half = moved_high.shape[0] // 2
        return (
            self.move(moved_high[:half], lambda d: d & 1 == 1, lambda r: r ^ 1),
            self.move(moved_low[half:], lambda d: d & 1 == 0, lambda r: r ^ self.ratio),
        )

    def rest(self, blocks):
        full = []
        for holder, others in blocks:
            other = others[0] if len(others) == 1 else jnp.concatenate(others)
            full.append(jnp.where(self.away & 1 == 0, holder, other))
        for bit in bits_of(self.ratio)[1:]:
            full += [swap(value, "row", bit) for value in full]
        return [(value, (value,)) for value in full[2:]]


def broadcast_col(value):
    col_n = lax.axis_size("col")
    col = lax.axis_index("col")
    for bit in bits_of(col_n):
        moved = lax.ppermute(value, "col", [(i, i + bit) for i in range(bit)])
        value = jnp.where((col >= bit) & (col < 2 * bit), moved, value)
    return value


def body(panel_block, trailing):
    shard_rows, width = panel_block.shape
    half = shard_rows // 2
    row, col = lax.axis_index("row"), lax.axis_index("col")
    row_bits, col_bits = bits_of(lax.axis_size("row")), bits_of(lax.axis_size("col"))
    gather = Gather()
    ratio = gather.ratio
    low = row % ratio
    lane = jnp.arange(width)

    def identity_rows(first):
        return ((first + jnp.arange(shard_rows))[:, None] == lane).astype(F32)

    def index_of(part):
        return jnp.stack([part ^ low, gather.away & 1]).astype(jnp.int32)

    relayed = gather.relay(panel_block)
    gram = sum_small(dot_tn(panel_block, panel_block), "row", row_bits[:1])
    gram = sum_small(after(gram, relayed), "row", row_bits[1:])
    moved_high, moved_low = gather.near(after(relayed, gram))
    first_factor, first_inverse, first_basis, second = first_pass(gram, panel_block)

    second = sum_small(after(second, moved_high, moved_low), "row", row_bits)
    parts = [(relayed, (moved_high,))]
    raw, basis = product(
        index_of(0), trailing, first_inverse, jnp.zeros((shard_rows, width), F32), *parts[0]
    )
    bases = [basis]
    parts.append((moved_low, gather.across(*lax.optimization_barrier((moved_high, moved_low, second))[:2])))
    second_upper, second_inverse = second_pass(second)
    parts += gather.rest(parts)
    for part in range(1, ratio):
        raw, basis = product(index_of(part), trailing, first_inverse, raw, *parts[part])
        bases.append(basis)

    mine = col & 1
    give, keep = applied_halves(
        jnp.stack([mine, col]).astype(jnp.int32), raw, second_inverse, trailing
    )
    vectors = dot_nt(first_basis, second_inverse) + identity_rows(row * shard_rows)
    own_vectors = lax.dynamic_slice_in_dim(vectors, mine * half, half, 0)
    other_vectors = lax.dynamic_slice_in_dim(vectors, (1 - mine) * half, half, 0)
    inner = dot_tn(own_vectors, keep) + dot_tn(other_vectors, give)
    keep = keep + swap(give, "col", col_bits[0])
    inner = sum_small(inner, "row", row_bits)
    for bit in col_bits[1:]:
        keep = keep + swap(keep, "col", bit)
    other = swap(keep, "col", col_bits[0])
    applied = jnp.zeros((shard_rows, width), F32)
    applied = lax.dynamic_update_slice_in_dim(applied, keep, mine * half, 0)
    applied = lax.dynamic_update_slice_in_dim(applied, other, (1 - mine) * half, 0)

    relayed = gather.relay(after(applied, inner))
    inner = sum_small(inner, "col", col_bits)
    top = broadcast_col(
        sum(jnp.where(low == part, basis[:width], 0.0) for part, basis in enumerate(bases))
    )
    band_block, kernel = small_pass(second_upper, second_inverse, first_factor, top)
    inner = dot_tn(kernel, dot_nn(inner, kernel))
    left = jnp.concatenate(
        [dot_nt(vectors, kernel), dot_nn(applied, kernel) - dot_nn(vectors, inner)], axis=1
    )
    block_vectors = [
        dot_nt(basis, second_inverse) + identity_rows((col * ratio + (part ^ low)) * shard_rows)
        for part, basis in enumerate(bases)
    ]
    moved_high, moved_low = gather.near(relayed)
    parts = [(relayed, (moved_high,)), (moved_low, gather.across(moved_high, moved_low))]
    reduced = update(index_of(0), trailing, left, block_vectors[0], *parts[0], None)
    parts += gather.rest(parts)
    for part in range(1, ratio):
        reduced = update(index_of(part), trailing, left, block_vectors[part], *parts[part], reduced)
    return (reduced, band_block, first_factor)


def solution(mesh):
    in_specs = (P("row", None), P("row", "col"))
    out_specs = (P("row", "col"), P(), P())
    return jax.shard_map(body, mesh=mesh, in_specs=in_specs, out_specs=out_specs, check_vma=False)
```

```python
import functools

import jax
import jax.numpy as jnp
from jax import lax
from jax.experimental import pallas as pl
from jax.experimental.pallas import tpu as pltpu
from jax.sharding import PartitionSpec as P

HIGH = lax.Precision.HIGHEST
F32 = jnp.float32
BF16 = jnp.bfloat16
SUB = 8


def dot_nn(a, b):
    return lax.dot_general(a, b, (((1,), (0,)), ((), ())), precision=HIGH, preferred_element_type=F32)


def dot_nt(a, b):
    return lax.dot_general(a, b, (((1,), (1,)), ((), ())), precision=HIGH, preferred_element_type=F32)


def dot_tn(a, b):
    return lax.dot_general(a, b, (((0,), (0,)), ((), ())), precision=HIGH, preferred_element_type=F32)


def dot_fast(a, b):
    return lax.dot_general(a, b, (((1,), (0,)), ((), ())), preferred_element_type=F32)


def lane_copy(tile, lane):
    return jnp.broadcast_to(tile[:, lane : lane + 1], tile.shape)


def row_copy(tile, row):
    return jnp.broadcast_to(tile[row : row + 1, :], tile.shape)


def cholesky_tiles(tiles):
    size = tiles[0].shape[1]
    count = len(tiles)
    tiles = list(tiles)
    lanes = lax.broadcasted_iota(jnp.int32, (SUB, size), 1)
    subs = lax.broadcasted_iota(jnp.int32, (SUB, size), 0)
    upper, inverse = [], []
    for block in range(count):
        base = block * SUB
        here = (lanes >= base) & (lanes < base + SUB)
        columns = [[lane_copy(tiles[i], base + k) for k in range(SUB)] for i in range(block, count)]
        right = jnp.where(lanes >= base, tiles[block], 0.0)
        left = jnp.where(lanes < base, tiles[block], 0.0)
        left = jnp.where(lanes - base == subs, 1.0, left)
        out_upper, out_inverse = jnp.zeros_like(right), jnp.zeros_like(left)
        below = [jnp.where(here, 0.0, tiles[i]) for i in range(block + 1, count)]
        for k in range(SUB):
            diag = columns[0]
            pivot = row_copy(diag[k], k)
            root = lax.rsqrt(pivot)
            recip = 1.0 / pivot
            right_row, left_row = row_copy(right, k), row_copy(left, k)
            out_upper = jnp.where(subs == k, right_row * root, out_upper)
            out_inverse = jnp.where(subs == k, left_row * root, out_inverse)
            packed = jnp.where(lanes < base + SUB, left_row, right_row) * recip
            rows = {l: row_copy(diag[l], k) * recip for l in range(k + 1, SUB)}
            factor = jnp.where(subs > k, diag[k], 0.0)
            right = right - factor * (right_row * recip)
            left = left - factor * (left_row * recip)
            for i in range(count - block):
                for l in range(k + 1, SUB):
                    if i == 0:
                        columns[0][l] = columns[0][l] - factor * rows[l]
                    else:
                        columns[i][l] = columns[i][l] - columns[i][k] * rows[l]
                if i:
                    below[i - 1] = below[i - 1] - columns[i][k] * packed
        for i in range(block + 1, count):
            tiles[i] = below[i - block - 1]
        upper.append(jnp.where(lanes >= base + subs, out_upper, 0.0))
        inverse.append(out_inverse)
    return upper, inverse


def invert_tiles(tiles):
    size = tiles[0].shape[1]
    count = len(tiles)
    tiles = list(tiles)
    lanes = lax.broadcasted_iota(jnp.int32, (SUB, size), 1)
    subs = lax.broadcasted_iota(jnp.int32, (SUB, size), 0)
    for block in range(count):
        base = block * SUB
        here = (lanes >= base) & (lanes < base + SUB)
        columns = [[lane_copy(tiles[i], base + k) for k in range(SUB)] for i in range(count)]
        diag = list(columns[block])
        row = jnp.where(here, jnp.where(lanes - base == subs, 1.0, 0.0), tiles[block])
        for k in range(SUB):
            recip = 1.0 / row_copy(diag[k], k)
            own = subs == k
            pivot_row = row_copy(row, k) * recip
            rows = {l: row_copy(diag[l], k) * recip for l in range(k + 1, SUB)}
            row = jnp.where(own, pivot_row, row - diag[k] * pivot_row)
            for l in range(k + 1, SUB):
                diag[l] = jnp.where(own, rows[l], diag[l] - diag[k] * rows[l])
        spread = [row_copy(row, k) for k in range(SUB)]
        for i in range(count):
            if i == block:
                continue
            value = jnp.where(here, 0.0, tiles[i])
            for k in range(SUB):
                value = value - columns[i][k] * spread[k]
            tiles[i] = value
        tiles[block] = row
    return tiles


def tiles_of(ref):
    return [ref[i * SUB : (i + 1) * SUB, :] for i in range(ref.shape[0] // SUB)]


def first_kernel(gram_ref, panel_ref, factor_ref, inverse_ref, basis_ref, second_ref):
    upper, inverse = cholesky_tiles(tiles_of(gram_ref))
    factor_ref[...] = jnp.concatenate(upper, axis=0).T
    inverse_ref[...] = jnp.concatenate(inverse, axis=0)
    basis_ref[...] = dot_nt(panel_ref[...], inverse_ref[...])
    basis = basis_ref[...]
    second_ref[...] = dot_tn(basis, basis)


def first_pass(gram, panel):
    square = jax.ShapeDtypeStruct(gram.shape, F32)
    return pl.pallas_call(
        first_kernel,
        out_shape=(square, square, jax.ShapeDtypeStruct(panel.shape, F32), square),
        compiler_params=pltpu.CompilerParams(vmem_limit_bytes=24 * 1024 * 1024),
        name="first_pass",
    )(gram, panel)


def second_kernel(gram_ref, upper_ref, inverse_ref):
    upper, inverse = cholesky_tiles(tiles_of(gram_ref))
    upper_ref[...] = jnp.concatenate(upper, axis=0)
    inverse_ref[...] = jnp.concatenate(inverse, axis=0)


def second_pass(gram):
    square = jax.ShapeDtypeStruct(gram.shape, F32)
    return pl.pallas_call(
        second_kernel,
        out_shape=(square, square),
        compiler_params=pltpu.CompilerParams(vmem_limit_bytes=8 * 1024 * 1024),
        name="second_pass",
    )(gram)


def small_kernel(upper_ref, inverse_ref, first_ref, top_ref, band_ref, kernel_ref):
    band_ref[...] = -dot_nt(upper_ref[...], first_ref[...])
    size = upper_ref.shape[0]
    rows = lax.broadcasted_iota(jnp.int32, (size, size), 0)
    lanes = lax.broadcasted_iota(jnp.int32, (size, size), 1)
    eye = jnp.where(rows == lanes, 1.0, 0.0)
    kernel_ref[...] = eye + dot_nt(inverse_ref[...], top_ref[...])
    kernel_ref[...] = jnp.concatenate(invert_tiles(tiles_of(kernel_ref)), axis=0)


def small_pass(upper, inverse, first_factor, top):
    square = jax.ShapeDtypeStruct(upper.shape, F32)
    return pl.pallas_call(
        small_kernel,
        out_shape=(square, square),
        compiler_params=pltpu.CompilerParams(vmem_limit_bytes=8 * 1024 * 1024),
        name="small_pass",
    )(upper, inverse, first_factor, top)


def split(value):
    high = value.astype(BF16)
    return high, (value - high.astype(F32)).astype(BF16)


def fetch(away, holder, other, into, sem):
    @pl.when(away == 0)
    def _():
        copy = pltpu.make_async_copy(holder, into, sem)
        copy.start()
        copy.wait()

    @pl.when(away != 0)
    def _():
        copy = pltpu.make_async_copy(other, into, sem)
        copy.start()
        copy.wait()


def chunk_of(rows):
    return min(rows, 256)


def product_kernel(
    index_ref, trailing, inverse_ref, before_ref, holder_ref, other_ref,
    out_ref, basis_ref, tiles, panel, both, sem, sems,
):
    slots, chunk, depth = tiles.shape
    rows, width = out_ref.shape
    count = rows // chunk
    columns = pl.ds(pl.multiple_of(index_ref[0] * depth, depth), depth)

    def load(i):
        part = pl.ds(pl.multiple_of(i * chunk, chunk), chunk)
        slot = i % slots
        return pltpu.make_async_copy(trailing.at[part, columns], tiles.at[slot], sems.at[slot])

    for i in range(slots):
        load(i).start()

    fetch(index_ref[1], holder_ref, other_ref, panel, sem)
    basis_ref[...] = dot_nt(panel[...], inverse_ref[...])
    high, low = split(basis_ref[...])
    both[:, :width] = high
    both[:, width:] = low

    @pl.loop(0, rows // chunk)
    def _(i):
        load(i).wait()
        part = pl.ds(pl.multiple_of(i * chunk, chunk), chunk)
        high, low = split(tiles[i % slots])
        right = both[...]
        value = dot_fast(high, right) + dot_fast(low, right)
        out_ref[part, :] = before_ref[part, :] + (value[:, :width] + value[:, width:])

        @pl.when(i + slots < count)
        def _():
            load(i + slots).start()


def product(index, trailing, inverse, before, holder, other):
    rows = trailing.shape[0]
    depth, width = holder.shape
    chunk = chunk_of(rows)
    slots = min(4, rows // chunk)
    anywhere = pl.BlockSpec(memory_space=pl.ANY)
    near = pl.BlockSpec(memory_space=pltpu.VMEM)
    return pl.pallas_call(
        product_kernel,
        out_shape=(
            jax.ShapeDtypeStruct((rows, width), F32),
            jax.ShapeDtypeStruct((depth, width), F32),
        ),
        in_specs=[
            pl.BlockSpec(memory_space=pltpu.SMEM),
            anywhere,
            near,
            near,
            anywhere,
            anywhere,
        ],
        out_specs=(near, near),
        scratch_shapes=[
            pltpu.VMEM((slots, chunk, depth), F32),
            pltpu.VMEM((depth, width), F32),
            pltpu.VMEM((depth, 2 * width), BF16),
            pltpu.SemaphoreType.DMA,
            pltpu.SemaphoreType.DMA((slots,)),
        ],
        compiler_params=pltpu.CompilerParams(vmem_limit_bytes=20 * 1024 * 1024),
        cost_estimate=pl.CostEstimate(
            flops=8 * rows * depth * width, bytes_accessed=4 * rows * depth, transcendentals=0
        ),
        name="product",
    )(index, trailing, inverse, before, holder, other)


def update_kernel(
    index_ref, trailing, left_ref, vectors_ref, holder_ref, other_ref, _,
    out, tiles, applied, right, sem, loads, stores,
):
    slots, chunk, depth = tiles.shape
    rows, width = left_ref.shape[0], vectors_ref.shape[1]
    count = rows // chunk
    ahead = max(slots - 2, 1)
    columns = pl.ds(pl.multiple_of(index_ref[0] * depth, depth), depth)

    def load(i):
        part = pl.ds(pl.multiple_of(i * chunk, chunk), chunk)
        slot = i % slots
        return pltpu.make_async_copy(trailing.at[part, columns], tiles.at[slot], loads.at[slot])

    def store(i):
        part = pl.ds(pl.multiple_of(i * chunk, chunk), chunk)
        slot = i % slots
        return pltpu.make_async_copy(tiles.at[slot], out.at[part, columns], stores.at[slot])

    for i in range(min(ahead, count)):
        load(i).start()

    fetch(index_ref[1], holder_ref, other_ref, applied, sem)
    for place, ref in ((0, applied), (width, vectors_ref)):
        high, low = split(ref[...].T)
        right[place : place + width, :] = high
        right[2 * width + place : 3 * width + place, :] = low
        right[4 * width + place : 5 * width + place, :] = high

    @pl.loop(0, count)
    def _(i):
        @pl.when(i + ahead < count)
        def _():
            @pl.when(i + ahead >= slots)
            def _():
                store(i + ahead - slots).wait()

            load(i + ahead).start()

        load(i).wait()
        part = pl.ds(pl.multiple_of(i * chunk, chunk), chunk)
        high, low = split(left_ref[part, :])
        left = jnp.concatenate([high, high, low], axis=1)
        slot = i % slots
        tiles[slot] = tiles[slot] - dot_fast(left, right[...])
        store(i).start()

    for i in range(max(count - slots, 0), count):
        store(i).wait()


def update(index, trailing, left, vectors, holder, other, reduced):
    rows = trailing.shape[0]
    depth, width = vectors.shape
    chunk = chunk_of(rows)
    slots = min(5, rows // chunk)
    anywhere = pl.BlockSpec(memory_space=pl.ANY)
    near = pl.BlockSpec(memory_space=pltpu.VMEM)
    aliases = {}
    if reduced is None:
        reduced = index
    else:
        aliases = {6: 0}
    return pl.pallas_call(
        update_kernel,
        out_shape=jax.ShapeDtypeStruct(trailing.shape, F32),
        in_specs=[
            pl.BlockSpec(memory_space=pltpu.SMEM),
            anywhere,
            near,
            near,
            anywhere,
            anywhere,
            anywhere,
        ],
        out_specs=anywhere,
        scratch_shapes=[
            pltpu.VMEM((slots, chunk, depth), F32),
            pltpu.VMEM((depth, width), F32),
            pltpu.VMEM((6 * width, depth), BF16),
            pltpu.SemaphoreType.DMA,
            pltpu.SemaphoreType.DMA((slots,)),
            pltpu.SemaphoreType.DMA((slots,)),
        ],
        input_output_aliases=aliases,
        compiler_params=pltpu.CompilerParams(vmem_limit_bytes=26 * 1024 * 1024),
        cost_estimate=pl.CostEstimate(
            flops=12 * rows * depth * width, bytes_accessed=8 * rows * depth, transcendentals=0
        ),
        name="update",
    )(index, trailing, left, vectors, holder, other, reduced)


def dot_three(a, b, dims):
    a_high, a_low = split(a)
    b_high, b_low = split(b)
    dot = lambda x, y: lax.dot_general(x, y, (dims, ((), ())), preferred_element_type=F32)
    return dot(a_high, b_high) + (dot(a_high, b_low) + dot(a_low, b_high))


def applied_kernel(
    index_ref, raw_ref, basis_ref, inverse_ref, lead_ref, give_ref, keep_ref, vectors_ref, inner_ref
):
    step = pl.program_id(0)
    half, width = raw_ref.shape
    value = dot_three(raw_ref[...], inverse_ref[...], ((1,), (1,)))
    value = value + jnp.where(index_ref[1] == 0, lead_ref[...], 0.0)
    first = index_ref[2] + (1 - (index_ref[0] ^ step)) * half
    rows = lax.broadcasted_iota(jnp.int32, (half, width), 0) + first
    lanes = lax.broadcasted_iota(jnp.int32, (half, width), 1)
    vectors = dot_three(basis_ref[...], inverse_ref[...], ((1,), (1,)))
    vectors = vectors + jnp.where(rows == lanes, 1.0, 0.0)
    vectors_ref[...] = vectors
    inner = dot_three(vectors, value, ((0,), (0,)))

    @pl.when(step == 0)
    def _():
        give_ref[...] = value
        inner_ref[...] = inner

    @pl.when(step == 1)
    def _():
        keep_ref[...] = value
        inner_ref[...] += inner


def applied_halves(index, raw, basis, inverse, trailing):
    rows, width = raw.shape
    half = rows // 2
    whole = pl.BlockSpec((half, width), lambda i, index: (0, 0))
    square = pl.BlockSpec((width, width), lambda i, index: (0, 0))
    piece = pl.BlockSpec((half, width), lambda i, index: (1 - (index[0] ^ i), 0))
    out = jax.ShapeDtypeStruct((half, width), F32)
    return pl.pallas_call(
        applied_kernel,
        out_shape=(
            out,
            out,
            jax.ShapeDtypeStruct((rows, width), F32),
            jax.ShapeDtypeStruct((width, width), F32),
        ),
        grid_spec=pltpu.PrefetchScalarGridSpec(
            num_scalar_prefetch=1,
            grid=(2,),
            in_specs=[piece, piece, square, piece],
            out_specs=(whole, whole, piece, square),
        ),
        compiler_params=pltpu.CompilerParams(vmem_limit_bytes=24 * 1024 * 1024),
        name="applied",
    )(index, raw, basis, inverse, trailing)


def after(value, *others):
    return lax.optimization_barrier((value, *others))[0]


def swap(value, axis, bit):
    count = lax.axis_size(axis)
    return lax.ppermute(value, axis, [(i, i ^ bit) for i in range(count)])


def bits_of(count):
    return [1 << b for b in range(count.bit_length() - 1)]


def sum_small(value, axis, bits):
    for bit in bits:
        value = value + swap(value, axis, bit)
    return value


class Gather:
    def __init__(self):
        self.row_n, self.col_n = lax.axis_size("row"), lax.axis_size("col")
        self.ratio = self.row_n // self.col_n
        self.away = (lax.axis_index("row") // self.ratio) ^ lax.axis_index("col")

    def move(self, value, holds, to_row):
        pairs = []
        for r in range(self.row_n):
            for c in range(self.col_n):
                if holds((r // self.ratio) ^ c):
                    pairs.append((r * self.col_n + c, to_row(r) * self.col_n + c))
        return lax.ppermute(value, ("row", "col"), pairs)

    def relay(self, value, done=0):
        for bit in reversed(bits_of(self.col_n)[1:]):
            if bit & done:
                continue
            moved = self.move(
                value, lambda d: d & ~done == 0, lambda r: r ^ (bit * self.ratio)
            )
            value = jnp.where((self.away & ~done) == bit, moved, value)
            done |= bit
        return value

    def relay_halves(self, value, meanwhile):
        bit = self.col_n // 2
        half = value.shape[0] // 2
        across = (self.away == bit).astype(jnp.int32)
        piece = lax.dynamic_slice_in_dim(value, across * half, half, 0)
        first = self.move(piece, lambda d: d & ~bit == 0, lambda r: r ^ (bit * self.ratio))
        first, meanwhile = lax.optimization_barrier((first, meanwhile))
        pairs = []
        for r in range(self.row_n):
            c = r // self.ratio
            pairs.append((r * self.col_n + c, r * self.col_n + (c ^ bit)))
        second = lax.ppermute(first, ("row", "col"), pairs)
        moved = jnp.concatenate([first, second])
        return jnp.where(self.away == bit, moved, value), meanwhile

    def near(self, value):
        holds = lambda d: d & 1 == 0
        return (
            self.move(value, holds, lambda r: r ^ self.ratio),
            self.move(value, holds, lambda r: r ^ 1),
        )

    def across(self, moved_high):
        return self.move(moved_high, lambda d: d & 1 == 1, lambda r: r ^ 1)

    def rest(self, blocks):
        full = []
        for holder, other in blocks:
            full.append(jnp.where(self.away & 1 == 0, holder, other))
        for bit in bits_of(self.ratio)[1:]:
            full += [swap(value, "row", bit) for value in full]
        return [(value, value) for value in full[2:]]


def broadcast_col(value):
    col_n = lax.axis_size("col")
    col = lax.axis_index("col")
    for bit in bits_of(col_n):
        moved = lax.ppermute(value, "col", [(i, i + bit) for i in range(bit)])
        value = jnp.where((col >= bit) & (col < 2 * bit), moved, value)
    return value


def body(panel_block, trailing):
    shard_rows, width = panel_block.shape
    half = shard_rows // 2
    row, col = lax.axis_index("row"), lax.axis_index("col")
    row_bits, col_bits = bits_of(lax.axis_size("row")), bits_of(lax.axis_size("col"))
    gather = Gather()
    ratio = gather.ratio
    low = row % ratio
    lane = jnp.arange(width)

    def identity_rows(first):
        return ((first + jnp.arange(shard_rows))[:, None] == lane).astype(F32)

    def index_of(part):
        return jnp.stack([part ^ low, gather.away & 1]).astype(jnp.int32)

    gram = sum_small(dot_tn(panel_block, panel_block), "row", row_bits[:1])
    relayed, gram = gather.relay_halves(panel_block, gram)
    relayed = gather.relay(relayed, lax.axis_size("col") // 2)
    gram = sum_small(gram, "row", row_bits[1:])
    moved_high, moved_low = gather.near(after(relayed, gram))
    first_factor, first_inverse, first_basis, second = first_pass(gram, panel_block)

    moved_high, second = lax.optimization_barrier((moved_high, second))
    parts = [(relayed, moved_high), (moved_low, gather.across(moved_high))]
    raw, basis = product(
        index_of(0), trailing, first_inverse, jnp.zeros((shard_rows, width), F32), *parts[0]
    )
    bases = [basis]
    second = sum_small(second, "row", row_bits[::-1])
    parts += gather.rest(parts)
    for part in range(1, ratio):
        raw, basis = product(index_of(part), trailing, first_inverse, raw, *parts[part])
        bases.append(basis)
    second_upper, second_inverse = second_pass(second)

    mine = col & 1
    give, keep, vectors, inner = applied_halves(
        jnp.stack([mine, col, row * shard_rows]).astype(jnp.int32),
        raw,
        first_basis,
        second_inverse,
        trailing,
    )
    keep = keep + swap(give, "col", col_bits[0])
    inner = sum_small(inner, "row", row_bits)
    for bit in col_bits[1:]:
        moved, inner = lax.optimization_barrier((swap(keep, "col", bit), inner))
        keep = keep + moved
    other = swap(keep, "col", col_bits[0])
    applied = jnp.zeros((shard_rows, width), F32)
    applied = lax.dynamic_update_slice_in_dim(applied, keep, mine * half, 0)
    applied = lax.dynamic_update_slice_in_dim(applied, other, (1 - mine) * half, 0)

    relayed = gather.relay(applied)
    inner = sum_small(inner, "col", col_bits)
    top = sum(jnp.where(low == part, basis[:width], 0.0) for part, basis in enumerate(bases))
    top = broadcast_col(after(top, applied))
    band_block, kernel = small_pass(second_upper, second_inverse, first_factor, top)
    inner = dot_tn(kernel, dot_nn(inner, kernel))
    left = jnp.concatenate(
        [dot_nt(vectors, kernel), dot_nn(applied, kernel) - dot_nn(vectors, inner)], axis=1
    )
    block_vectors = [
        dot_nt(basis, second_inverse) + identity_rows((col * ratio + (part ^ low)) * shard_rows)
        for part, basis in enumerate(bases)
    ]
    moved_high, moved_low = gather.near(relayed)
    parts = [(relayed, moved_high), (moved_low, gather.across(moved_high))]
    reduced = update(index_of(0), trailing, left, block_vectors[0], *parts[0], None)
    parts += gather.rest(parts)
    for part in range(1, ratio):
        reduced = update(index_of(part), trailing, left, block_vectors[part], *parts[part], reduced)
    return (reduced, band_block, first_factor)


def solution(mesh):
    in_specs = (P("row", None), P("row", "col"))
    out_specs = (P("row", "col"), P(), P())
    return jax.shard_map(body, mesh=mesh, in_specs=in_specs, out_specs=out_specs, check_vma=False)
```

```python
import functools

import jax
import jax.numpy as jnp
from jax import lax
from jax.experimental import pallas as pl
from jax.experimental.pallas import tpu as pltpu
from jax.sharding import PartitionSpec as P

HIGH = lax.Precision.HIGHEST
F32 = jnp.float32
BF16 = jnp.bfloat16
SUB = 8


def dot_nn(a, b):
    return lax.dot_general(a, b, (((1,), (0,)), ((), ())), precision=HIGH, preferred_element_type=F32)


def dot_nt(a, b):
    return lax.dot_general(a, b, (((1,), (1,)), ((), ())), precision=HIGH, preferred_element_type=F32)


def dot_tn(a, b):
    return lax.dot_general(a, b, (((0,), (0,)), ((), ())), precision=HIGH, preferred_element_type=F32)


def dot_fast(a, b):
    return lax.dot_general(a, b, (((1,), (0,)), ((), ())), preferred_element_type=F32)


def lane_copy(tile, lane):
    return jnp.broadcast_to(tile[:, lane : lane + 1], tile.shape)


def row_copy(tile, row):
    return jnp.broadcast_to(tile[row : row + 1, :], tile.shape)


def cholesky_tiles(tiles):
    size = tiles[0].shape[1]
    count = len(tiles)
    tiles = list(tiles)
    lanes = lax.broadcasted_iota(jnp.int32, (SUB, size), 1)
    subs = lax.broadcasted_iota(jnp.int32, (SUB, size), 0)
    upper, inverse = [], []
    for block in range(count):
        base = block * SUB
        here = (lanes >= base) & (lanes < base + SUB)
        columns = [[lane_copy(tiles[i], base + k) for k in range(SUB)] for i in range(block, count)]
        right = jnp.where(lanes >= base, tiles[block], 0.0)
        left = jnp.where(lanes < base, tiles[block], 0.0)
        left = jnp.where(lanes - base == subs, 1.0, left)
        out_upper, out_inverse = jnp.zeros_like(right), jnp.zeros_like(left)
        below = [jnp.where(here, 0.0, tiles[i]) for i in range(block + 1, count)]
        for k in range(SUB):
            diag = columns[0]
            pivot = row_copy(diag[k], k)
            root = lax.rsqrt(pivot)
            recip = 1.0 / pivot
            right_row, left_row = row_copy(right, k), row_copy(left, k)
            out_upper = jnp.where(subs == k, right_row * root, out_upper)
            out_inverse = jnp.where(subs == k, left_row * root, out_inverse)
            packed = jnp.where(lanes < base + SUB, left_row, right_row) * recip
            rows = {l: row_copy(diag[l], k) * recip for l in range(k + 1, SUB)}
            factor = jnp.where(subs > k, diag[k], 0.0)
            right = right - factor * (right_row * recip)
            left = left - factor * (left_row * recip)
            for i in range(count - block):
                for l in range(k + 1, SUB):
                    if i == 0:
                        columns[0][l] = columns[0][l] - factor * rows[l]
                    else:
                        columns[i][l] = columns[i][l] - columns[i][k] * rows[l]
                if i:
                    below[i - 1] = below[i - 1] - columns[i][k] * packed
        for i in range(block + 1, count):
            tiles[i] = below[i - block - 1]
        upper.append(jnp.where(lanes >= base + subs, out_upper, 0.0))
        inverse.append(out_inverse)
    return upper, inverse


def invert_tiles(tiles):
    size = tiles[0].shape[1]
    count = len(tiles)
    tiles = list(tiles)
    lanes = lax.broadcasted_iota(jnp.int32, (SUB, size), 1)
    subs = lax.broadcasted_iota(jnp.int32, (SUB, size), 0)
    for block in range(count):
        base = block * SUB
        here = (lanes >= base) & (lanes < base + SUB)
        columns = [[lane_copy(tiles[i], base + k) for k in range(SUB)] for i in range(count)]
        diag = list(columns[block])
        row = jnp.where(here, jnp.where(lanes - base == subs, 1.0, 0.0), tiles[block])
        for k in range(SUB):
            recip = 1.0 / row_copy(diag[k], k)
            own = subs == k
            pivot_row = row_copy(row, k) * recip
            rows = {l: row_copy(diag[l], k) * recip for l in range(k + 1, SUB)}
            row = jnp.where(own, pivot_row, row - diag[k] * pivot_row)
            for l in range(k + 1, SUB):
                diag[l] = jnp.where(own, rows[l], diag[l] - diag[k] * rows[l])
        spread = [row_copy(row, k) for k in range(SUB)]
        for i in range(count):
            if i == block:
                continue
            value = jnp.where(here, 0.0, tiles[i])
            for k in range(SUB):
                value = value - columns[i][k] * spread[k]
            tiles[i] = value
        tiles[block] = row
    return tiles


def tiles_of(ref):
    return [ref[i * SUB : (i + 1) * SUB, :] for i in range(ref.shape[0] // SUB)]


def first_kernel(gram_ref, panel_ref, factor_ref, inverse_ref, basis_ref, second_ref):
    upper, inverse = cholesky_tiles(tiles_of(gram_ref))
    factor_ref[...] = jnp.concatenate(upper, axis=0).T
    inverse_ref[...] = jnp.concatenate(inverse, axis=0)
    basis_ref[...] = dot_nt(panel_ref[...], inverse_ref[...])
    basis = basis_ref[...]
    second_ref[...] = dot_tn(basis, basis)


def first_pass(gram, panel):
    square = jax.ShapeDtypeStruct(gram.shape, F32)
    return pl.pallas_call(
        first_kernel,
        out_shape=(square, square, jax.ShapeDtypeStruct(panel.shape, F32), square),
        compiler_params=pltpu.CompilerParams(vmem_limit_bytes=24 * 1024 * 1024),
        name="first_pass",
    )(gram, panel)


def second_kernel(gram_ref, upper_ref, inverse_ref):
    upper, inverse = cholesky_tiles(tiles_of(gram_ref))
    upper_ref[...] = jnp.concatenate(upper, axis=0)
    inverse_ref[...] = jnp.concatenate(inverse, axis=0)


def second_pass(gram):
    square = jax.ShapeDtypeStruct(gram.shape, F32)
    return pl.pallas_call(
        second_kernel,
        out_shape=(square, square),
        compiler_params=pltpu.CompilerParams(vmem_limit_bytes=8 * 1024 * 1024),
        name="second_pass",
    )(gram)


def small_kernel(upper_ref, inverse_ref, first_ref, top_ref, band_ref, kernel_ref):
    band_ref[...] = -dot_nt(upper_ref[...], first_ref[...])
    size = upper_ref.shape[0]
    rows = lax.broadcasted_iota(jnp.int32, (size, size), 0)
    lanes = lax.broadcasted_iota(jnp.int32, (size, size), 1)
    eye = jnp.where(rows == lanes, 1.0, 0.0)
    kernel_ref[...] = eye + dot_nt(inverse_ref[...], top_ref[...])
    kernel_ref[...] = jnp.concatenate(invert_tiles(tiles_of(kernel_ref)), axis=0)


def small_pass(upper, inverse, first_factor, top):
    square = jax.ShapeDtypeStruct(upper.shape, F32)
    return pl.pallas_call(
        small_kernel,
        out_shape=(square, square),
        compiler_params=pltpu.CompilerParams(vmem_limit_bytes=8 * 1024 * 1024),
        name="small_pass",
    )(upper, inverse, first_factor, top)


def split(value):
    high = value.astype(BF16)
    return high, (value - high.astype(F32)).astype(BF16)


def fetch(away, holder, other, into, sem):
    @pl.when(away == 0)
    def _():
        pltpu.make_async_copy(holder, into, sem).start()

    @pl.when(away != 0)
    def _():
        pltpu.make_async_copy(other, into, sem).start()

    return pltpu.make_async_copy(holder, into, sem)


def chunk_of(rows):
    return min(rows, 256)


def product_kernel(
    index_ref, trailing, inverse_ref, before_ref, holder_ref, other_ref,
    out_ref, basis_ref, tiles, panel, both, sem, sems,
):
    slots, chunk, depth = tiles.shape
    rows, width = out_ref.shape
    count = rows // chunk
    columns = pl.ds(pl.multiple_of(index_ref[0] * depth, depth), depth)

    def load(i):
        part = pl.ds(pl.multiple_of(i * chunk, chunk), chunk)
        slot = i % slots
        return pltpu.make_async_copy(trailing.at[part, columns], tiles.at[slot], sems.at[slot])

    fetched = fetch(index_ref[1], holder_ref, other_ref, panel, sem)
    for i in range(slots):
        load(i).start()

    fetched.wait()
    basis_ref[...] = dot_nt(panel[...], inverse_ref[...])
    high, low = split(basis_ref[...])
    both[:, :width] = high
    both[:, width:] = low

    @pl.loop(0, rows // chunk)
    def _(i):
        load(i).wait()
        part = pl.ds(pl.multiple_of(i * chunk, chunk), chunk)
        high, low = split(tiles[i % slots])
        right = both[...]
        value = dot_fast(high, right) + dot_fast(low, right)
        out_ref[part, :] = before_ref[part, :] + (value[:, :width] + value[:, width:])

        @pl.when(i + slots < count)
        def _():
            load(i + slots).start()


def product(index, trailing, inverse, before, holder, other):
    rows = trailing.shape[0]
    depth, width = holder.shape
    chunk = chunk_of(rows)
    slots = min(4, rows // chunk)
    anywhere = pl.BlockSpec(memory_space=pl.ANY)
    near = pl.BlockSpec(memory_space=pltpu.VMEM)
    return pl.pallas_call(
        product_kernel,
        out_shape=(
            jax.ShapeDtypeStruct((rows, width), F32),
            jax.ShapeDtypeStruct((depth, width), F32),
        ),
        in_specs=[
            pl.BlockSpec(memory_space=pltpu.SMEM),
            anywhere,
            near,
            near,
            anywhere,
            anywhere,
        ],
        out_specs=(near, near),
        scratch_shapes=[
            pltpu.VMEM((slots, chunk, depth), F32),
            pltpu.VMEM((depth, width), F32),
            pltpu.VMEM((depth, 2 * width), BF16),
            pltpu.SemaphoreType.DMA,
            pltpu.SemaphoreType.DMA((slots,)),
        ],
        compiler_params=pltpu.CompilerParams(vmem_limit_bytes=28 * 1024 * 1024),
        cost_estimate=pl.CostEstimate(
            flops=8 * rows * depth * width, bytes_accessed=4 * rows * depth, transcendentals=0
        ),
        name="product",
    )(index, trailing, inverse, before, holder, other)


def update_kernel(
    index_ref, trailing, left_ref, vectors_ref, holder_ref, other_ref, _,
    out, tiles, applied, right, sem, loads, stores,
):
    slots, chunk, depth = tiles.shape
    rows, width = left_ref.shape[0], vectors_ref.shape[1]
    count = rows // chunk
    ahead = max(slots - 2, 1)
    columns = pl.ds(pl.multiple_of(index_ref[0] * depth, depth), depth)

    def load(i):
        part = pl.ds(pl.multiple_of(i * chunk, chunk), chunk)
        slot = i % slots
        return pltpu.make_async_copy(trailing.at[part, columns], tiles.at[slot], loads.at[slot])

    def store(i):
        part = pl.ds(pl.multiple_of(i * chunk, chunk), chunk)
        slot = i % slots
        return pltpu.make_async_copy(tiles.at[slot], out.at[part, columns], stores.at[slot])

    fetched = fetch(index_ref[1], holder_ref, other_ref, applied, sem)
    for i in range(min(ahead, count)):
        load(i).start()

    fetched.wait()
    for place, ref in ((0, applied), (width, vectors_ref)):
        high, low = split(ref[...].T)
        right[place : place + width, :] = high
        right[2 * width + place : 3 * width + place, :] = low
        right[4 * width + place : 5 * width + place, :] = high

    @pl.loop(0, count)
    def _(i):
        @pl.when(i + ahead < count)
        def _():
            @pl.when(i + ahead >= slots)
            def _():
                store(i + ahead - slots).wait()

            load(i + ahead).start()

        load(i).wait()
        part = pl.ds(pl.multiple_of(i * chunk, chunk), chunk)
        high, low = split(left_ref[part, :])
        left = jnp.concatenate([high, high, low], axis=1)
        slot = i % slots
        tiles[slot] = tiles[slot] - dot_fast(left, right[...])
        store(i).start()

    for i in range(max(count - slots, 0), count):
        store(i).wait()


def update(index, trailing, left, vectors, holder, other, reduced):
    rows = trailing.shape[0]
    depth, width = vectors.shape
    chunk = chunk_of(rows)
    slots = min(5, rows // chunk)
    anywhere = pl.BlockSpec(memory_space=pl.ANY)
    near = pl.BlockSpec(memory_space=pltpu.VMEM)
    aliases = {}
    if reduced is None:
        reduced = index
    else:
        aliases = {6: 0}
    return pl.pallas_call(
        update_kernel,
        out_shape=jax.ShapeDtypeStruct(trailing.shape, F32),
        in_specs=[
            pl.BlockSpec(memory_space=pltpu.SMEM),
            anywhere,
            near,
            near,
            anywhere,
            anywhere,
            anywhere,
        ],
        out_specs=anywhere,
        scratch_shapes=[
            pltpu.VMEM((slots, chunk, depth), F32),
            pltpu.VMEM((depth, width), F32),
            pltpu.VMEM((6 * width, depth), BF16),
            pltpu.SemaphoreType.DMA,
            pltpu.SemaphoreType.DMA((slots,)),
            pltpu.SemaphoreType.DMA((slots,)),
        ],
        input_output_aliases=aliases,
        compiler_params=pltpu.CompilerParams(vmem_limit_bytes=30 * 1024 * 1024),
        cost_estimate=pl.CostEstimate(
            flops=12 * rows * depth * width, bytes_accessed=8 * rows * depth, transcendentals=0
        ),
        name="update",
    )(index, trailing, left, vectors, holder, other, reduced)


def dot_three(a, b, dims):
    a_high, a_low = split(a)
    b_high, b_low = split(b)
    dot = lambda x, y: lax.dot_general(x, y, (dims, ((), ())), preferred_element_type=F32)
    return dot(a_high, b_high) + (dot(a_high, b_low) + dot(a_low, b_high))


def applied_kernel(
    index_ref, raw_ref, basis_ref, inverse_ref, lead_ref, give_ref, keep_ref, vectors_ref, inner_ref
):
    step = pl.program_id(0)
    half, width = raw_ref.shape
    value = dot_three(raw_ref[...], inverse_ref[...], ((1,), (1,)))
    value = value + jnp.where(index_ref[1] == 0, lead_ref[...], 0.0)
    first = index_ref[2] + (1 - (index_ref[0] ^ step)) * half
    rows = lax.broadcasted_iota(jnp.int32, (half, width), 0) + first
    lanes = lax.broadcasted_iota(jnp.int32, (half, width), 1)
    vectors = dot_three(basis_ref[...], inverse_ref[...], ((1,), (1,)))
    vectors = vectors + jnp.where(rows == lanes, 1.0, 0.0)
    vectors_ref[...] = vectors
    inner = dot_three(vectors, value, ((0,), (0,)))

    @pl.when(step == 0)
    def _():
        give_ref[...] = value
        inner_ref[...] = inner

    @pl.when(step == 1)
    def _():
        keep_ref[...] = value
        inner_ref[...] += inner


def applied_halves(index, raw, basis, inverse, trailing):
    rows, width = raw.shape
    half = rows // 2
    whole = pl.BlockSpec((half, width), lambda i, index: (0, 0))
    square = pl.BlockSpec((width, width), lambda i, index: (0, 0))
    piece = pl.BlockSpec((half, width), lambda i, index: (1 - (index[0] ^ i), 0))
    out = jax.ShapeDtypeStruct((half, width), F32)
    return pl.pallas_call(
        applied_kernel,
        out_shape=(
            out,
            out,
            jax.ShapeDtypeStruct((rows, width), F32),
            jax.ShapeDtypeStruct((width, width), F32),
        ),
        grid_spec=pltpu.PrefetchScalarGridSpec(
            num_scalar_prefetch=1,
            grid=(2,),
            in_specs=[piece, piece, square, piece],
            out_specs=(whole, whole, piece, square),
        ),
        compiler_params=pltpu.CompilerParams(vmem_limit_bytes=30 * 1024 * 1024),
        name="applied",
    )(index, raw, basis, inverse, trailing)


def after(value, *others):
    return lax.optimization_barrier((value, *others))[0]


def swap(value, axis, bit):
    count = lax.axis_size(axis)
    return lax.ppermute(value, axis, [(i, i ^ bit) for i in range(count)])


def bits_of(count):
    return [1 << b for b in range(count.bit_length() - 1)]


def sum_small(value, axis, bits):
    for bit in bits:
        value = value + swap(value, axis, bit)
    return value


class Gather:
    def __init__(self):
        self.row_n, self.col_n = lax.axis_size("row"), lax.axis_size("col")
        self.ratio = self.row_n // self.col_n
        self.away = (lax.axis_index("row") // self.ratio) ^ lax.axis_index("col")

    def move(self, value, holds, to_row):
        pairs = []
        for r in range(self.row_n):
            for c in range(self.col_n):
                if holds((r // self.ratio) ^ c):
                    pairs.append((r * self.col_n + c, to_row(r) * self.col_n + c))
        return lax.ppermute(value, ("row", "col"), pairs)

    def relay(self, value, done=0):
        for bit in reversed(bits_of(self.col_n)[1:]):
            if bit & done:
                continue
            moved = self.move(
                value, lambda d: d & ~done == 0, lambda r: r ^ (bit * self.ratio)
            )
            value = jnp.where((self.away & ~done) == bit, moved, value)
            done |= bit
        return value

    def second_half(self):
        return (self.away == self.col_n // 2).astype(jnp.int32)

    def relay_halves(self, value, piece, meanwhile):
        bit = self.col_n // 2
        first = self.move(piece, lambda d: d & ~bit == 0, lambda r: r ^ (bit * self.ratio))
        first, meanwhile = lax.optimization_barrier((first, meanwhile))
        pairs = []
        for r in range(self.row_n):
            c = r // self.ratio
            pairs.append((r * self.col_n + c, r * self.col_n + (c ^ bit)))
        second = lax.ppermute(first, ("row", "col"), pairs)
        moved = jnp.concatenate([first, second])
        return self.relay(jnp.where(self.away == bit, moved, value), bit), meanwhile

    def near(self, value):
        holds = lambda d: d & 1 == 0
        return (
            self.move(value, holds, lambda r: r ^ self.ratio),
            self.move(value, holds, lambda r: r ^ 1),
        )

    def across(self, moved_high):
        return self.move(moved_high, lambda d: d & 1 == 1, lambda r: r ^ 1)

    def rest(self, blocks):
        full = []
        for holder, other in blocks:
            full.append(jnp.where(self.away & 1 == 0, holder, other))
        for bit in bits_of(self.ratio)[1:]:
            full += [swap(value, "row", bit) for value in full]
        return [(value, value) for value in full[2:]]


def broadcast_col(value):
    col_n = lax.axis_size("col")
    col = lax.axis_index("col")
    for bit in bits_of(col_n):
        moved = lax.ppermute(value, "col", [(i, i + bit) for i in range(bit)])
        value = jnp.where((col >= bit) & (col < 2 * bit), moved, value)
    return value


def body(panel_block, trailing):
    shard_rows, width = panel_block.shape
    half = shard_rows // 2
    row, col = lax.axis_index("row"), lax.axis_index("col")
    row_bits, col_bits = bits_of(lax.axis_size("row")), bits_of(lax.axis_size("col"))
    gather = Gather()
    ratio = gather.ratio
    low = row % ratio
    lane = jnp.arange(width)

    def identity_rows(first):
        return ((first + jnp.arange(shard_rows))[:, None] == lane).astype(F32)

    def index_of(part):
        return jnp.stack([part ^ low, gather.away & 1]).astype(jnp.int32)

    gram = sum_small(dot_tn(panel_block, panel_block), "row", row_bits[:1])
    piece = lax.dynamic_slice_in_dim(panel_block, gather.second_half() * half, half, 0)
    relayed, gram = gather.relay_halves(panel_block, piece, gram)
    gram = sum_small(gram, "row", row_bits[1:])
    moved_high, moved_low = gather.near(after(relayed, gram))
    first_factor, first_inverse, first_basis, second = first_pass(gram, panel_block)

    second = sum_small(second, "row", row_bits[:1])
    moved_high, second = lax.optimization_barrier((moved_high, second))
    parts = [(relayed, moved_high), (moved_low, gather.across(moved_high))]
    raw, basis = product(
        index_of(0), trailing, first_inverse, jnp.zeros((shard_rows, width), F32), *parts[0]
    )
    bases = [basis]
    second = sum_small(second, "row", row_bits[:0:-1])
    parts += gather.rest(parts)
    for part in range(1, ratio):
        raw, basis = product(index_of(part), trailing, first_inverse, raw, *parts[part])
        bases.append(basis)
    second_upper, second_inverse = second_pass(second)

    mine = col & 1
    give, keep, vectors, inner = applied_halves(
        jnp.stack([mine, col, row * shard_rows]).astype(jnp.int32),
        raw,
        first_basis,
        second_inverse,
        trailing,
    )
    keep = keep + swap(give, "col", col_bits[0])
    inner = sum_small(inner, "row", row_bits)
    for bit in col_bits[1:]:
        moved, inner = lax.optimization_barrier((swap(keep, "col", bit), inner))
        keep = keep + moved
    keep = lax.optimization_barrier(keep)
    other = swap(keep, "col", col_bits[0])
    applied = jnp.zeros((shard_rows, width), F32)
    applied = lax.dynamic_update_slice_in_dim(applied, keep, mine * half, 0)
    applied = lax.dynamic_update_slice_in_dim(applied, other, (1 - mine) * half, 0)

    piece = jnp.where(mine == gather.second_half(), keep, other)
    top = sum(jnp.where(low == part, basis[:width], 0.0) for part, basis in enumerate(bases))
    top = broadcast_col(after(top, piece))
    band_block, kernel = small_pass(second_upper, second_inverse, first_factor, top)
    inner = sum_small(after(inner, piece), "col", col_bits)
    relayed, (inner, kernel) = gather.relay_halves(applied, piece, (inner, kernel))
    inner = dot_tn(kernel, dot_nn(inner, kernel))
    left = jnp.concatenate(
        [dot_nt(vectors, kernel), dot_nn(applied, kernel) - dot_nn(vectors, inner)], axis=1
    )
    block_vectors = [
        dot_nt(basis, second_inverse) + identity_rows((col * ratio + (part ^ low)) * shard_rows)
        for part, basis in enumerate(bases)
    ]
    relayed, left, *block_vectors = lax.optimization_barrier((relayed, left, *block_vectors))
    moved_high, moved_low = gather.near(relayed)
    parts = [(relayed, moved_high), (moved_low, gather.across(moved_high))]
    reduced = update(index_of(0), trailing, left, block_vectors[0], *parts[0], None)
    parts += gather.rest(parts)
    for part in range(1, ratio):
        reduced = update(index_of(part), trailing, left, block_vectors[part], *parts[part], reduced)
    return (reduced, band_block, first_factor)


def solution(mesh):
    in_specs = (P("row", None), P("row", "col"))
    out_specs = (P("row", "col"), P(), P())
    return jax.shard_map(body, mesh=mesh, in_specs=in_specs, out_specs=out_specs, check_vma=False)
```

```python
import functools

import jax
import jax.numpy as jnp
from jax import lax
from jax.experimental import pallas as pl
from jax.experimental.pallas import tpu as pltpu
from jax.sharding import PartitionSpec as P

HIGH = lax.Precision.HIGHEST
F32 = jnp.float32
BF16 = jnp.bfloat16
SUB = 8


def dot_nn(a, b):
    return lax.dot_general(a, b, (((1,), (0,)), ((), ())), precision=HIGH, preferred_element_type=F32)


def dot_nt(a, b):
    return lax.dot_general(a, b, (((1,), (1,)), ((), ())), precision=HIGH, preferred_element_type=F32)


def dot_tn(a, b):
    return lax.dot_general(a, b, (((0,), (0,)), ((), ())), precision=HIGH, preferred_element_type=F32)


def dot_fast(a, b):
    return lax.dot_general(a, b, (((1,), (0,)), ((), ())), preferred_element_type=F32)


def lane_copy(tile, lane):
    return jnp.broadcast_to(tile[:, lane : lane + 1], tile.shape)


def row_copy(tile, row):
    return jnp.broadcast_to(tile[row : row + 1, :], tile.shape)


def cholesky_tiles(tiles):
    size = tiles[0].shape[1]
    count = len(tiles)
    tiles = list(tiles)
    lanes = lax.broadcasted_iota(jnp.int32, (SUB, size), 1)
    subs = lax.broadcasted_iota(jnp.int32, (SUB, size), 0)
    upper, inverse = [], []
    for block in range(count):
        base = block * SUB
        here = (lanes >= base) & (lanes < base + SUB)
        columns = [[lane_copy(tiles[i], base + k) for k in range(SUB)] for i in range(block, count)]
        right = jnp.where(lanes >= base, tiles[block], 0.0)
        left = jnp.where(lanes < base, tiles[block], 0.0)
        left = jnp.where(lanes - base == subs, 1.0, left)
        out_upper, out_inverse = jnp.zeros_like(right), jnp.zeros_like(left)
        below = [jnp.where(here, 0.0, tiles[i]) for i in range(block + 1, count)]
        for k in range(SUB):
            diag = columns[0]
            pivot = row_copy(diag[k], k)
            root = lax.rsqrt(pivot)
            recip = 1.0 / pivot
            right_row, left_row = row_copy(right, k), row_copy(left, k)
            out_upper = jnp.where(subs == k, right_row * root, out_upper)
            out_inverse = jnp.where(subs == k, left_row * root, out_inverse)
            packed = jnp.where(lanes < base + SUB, left_row, right_row) * recip
            rows = {l: row_copy(diag[l], k) * recip for l in range(k + 1, SUB)}
            factor = jnp.where(subs > k, diag[k], 0.0)
            right = right - factor * (right_row * recip)
            left = left - factor * (left_row * recip)
            for i in range(count - block):
                for l in range(k + 1, SUB):
                    if i == 0:
                        columns[0][l] = columns[0][l] - factor * rows[l]
                    else:
                        columns[i][l] = columns[i][l] - columns[i][k] * rows[l]
                if i:
                    below[i - 1] = below[i - 1] - columns[i][k] * packed
        for i in range(block + 1, count):
            tiles[i] = below[i - block - 1]
        upper.append(jnp.where(lanes >= base + subs, out_upper, 0.0))
        inverse.append(out_inverse)
    return upper, inverse


def invert_tiles(tiles):
    size = tiles[0].shape[1]
    count = len(tiles)
    tiles = list(tiles)
    lanes = lax.broadcasted_iota(jnp.int32, (SUB, size), 1)
    subs = lax.broadcasted_iota(jnp.int32, (SUB, size), 0)
    for block in range(count):
        base = block * SUB
        here = (lanes >= base) & (lanes < base + SUB)
        columns = [[lane_copy(tiles[i], base + k) for k in range(SUB)] for i in range(count)]
        diag = list(columns[block])
        row = jnp.where(here, jnp.where(lanes - base == subs, 1.0, 0.0), tiles[block])
        for k in range(SUB):
            recip = 1.0 / row_copy(diag[k], k)
            own = subs == k
            pivot_row = row_copy(row, k) * recip
            rows = {l: row_copy(diag[l], k) * recip for l in range(k + 1, SUB)}
            row = jnp.where(own, pivot_row, row - diag[k] * pivot_row)
            for l in range(k + 1, SUB):
                diag[l] = jnp.where(own, rows[l], diag[l] - diag[k] * rows[l])
        spread = [row_copy(row, k) for k in range(SUB)]
        for i in range(count):
            if i == block:
                continue
            value = jnp.where(here, 0.0, tiles[i])
            for k in range(SUB):
                value = value - columns[i][k] * spread[k]
            tiles[i] = value
        tiles[block] = row
    return tiles


def tiles_of(ref):
    return [ref[i * SUB : (i + 1) * SUB, :] for i in range(ref.shape[0] // SUB)]


def split(value):
    high = value.astype(BF16)
    return high, (value - high.astype(F32)).astype(BF16)


def first_kernel(
    gram_ref, panel_ref, factor_ref, inverse_ref, basis_out, second_ref, basis_ref, sem
):
    upper, inverse = cholesky_tiles(tiles_of(gram_ref))
    inverse_ref[...] = jnp.concatenate(inverse, axis=0)
    basis_ref[...] = dot_nt(panel_ref[...], inverse_ref[...])
    copy = pltpu.make_async_copy(basis_ref, basis_out, sem)
    copy.start()
    factor_ref[...] = jnp.concatenate(upper, axis=0).T
    high, low = split(basis_ref[...])
    width = low.shape[1]
    value = lax.dot_general(
        high,
        jnp.concatenate([high, low], axis=1),
        (((0,), (0,)), ((), ())),
        preferred_element_type=F32,
    )
    cross = value[:, width:]
    second_ref[...] = value[:, :width] + (cross + cross.T)
    copy.wait()


def first_pass(gram, panel):
    square = jax.ShapeDtypeStruct(gram.shape, F32)
    near = pl.BlockSpec(memory_space=pltpu.VMEM)
    return pl.pallas_call(
        first_kernel,
        out_shape=(square, square, jax.ShapeDtypeStruct(panel.shape, F32), square),
        in_specs=[near, near],
        out_specs=(near, near, pl.BlockSpec(memory_space=pltpu.HBM), near),
        scratch_shapes=[pltpu.VMEM(panel.shape, F32), pltpu.SemaphoreType.DMA],
        compiler_params=pltpu.CompilerParams(vmem_limit_bytes=24 * 1024 * 1024),
        name="first_pass",
    )(gram, panel)


def second_kernel(gram_ref, upper_ref, inverse_ref):
    upper, inverse = cholesky_tiles(tiles_of(gram_ref))
    upper_ref[...] = jnp.concatenate(upper, axis=0)
    inverse_ref[...] = jnp.concatenate(inverse, axis=0)


def second_pass(gram):
    square = jax.ShapeDtypeStruct(gram.shape, F32)
    return pl.pallas_call(
        second_kernel,
        out_shape=(square, square),
        compiler_params=pltpu.CompilerParams(vmem_limit_bytes=8 * 1024 * 1024),
        name="second_pass",
    )(gram)


def small_kernel(upper_ref, inverse_ref, first_ref, top_ref, band_ref, kernel_ref):
    band_ref[...] = -dot_nt(upper_ref[...], first_ref[...])
    size = upper_ref.shape[0]
    rows = lax.broadcasted_iota(jnp.int32, (size, size), 0)
    lanes = lax.broadcasted_iota(jnp.int32, (size, size), 1)
    eye = jnp.where(rows == lanes, 1.0, 0.0)
    kernel_ref[...] = eye + dot_nt(inverse_ref[...], top_ref[...])
    kernel_ref[...] = jnp.concatenate(invert_tiles(tiles_of(kernel_ref)), axis=0)


def small_pass(upper, inverse, first_factor, top):
    square = jax.ShapeDtypeStruct(upper.shape, F32)
    return pl.pallas_call(
        small_kernel,
        out_shape=(square, square),
        compiler_params=pltpu.CompilerParams(vmem_limit_bytes=8 * 1024 * 1024),
        name="small_pass",
    )(upper, inverse, first_factor, top)


def fetch(away, holder, other, into, sem):
    @pl.when(away == 0)
    def _():
        pltpu.make_async_copy(holder, into, sem).start()

    @pl.when(away != 0)
    def _():
        pltpu.make_async_copy(other, into, sem).start()

    return pltpu.make_async_copy(holder, into, sem)


def product_kernel(
    index_ref, trailing, inverse_ref, before_ref, holder_ref, other_ref,
    out_ref, basis_out, tiles, panel, basis_ref, both, sem, sems,
):
    slots, chunk, depth = tiles.shape
    rows, width = out_ref.shape
    count = rows // chunk
    columns = pl.ds(pl.multiple_of(index_ref[0] * depth, depth), depth)

    def load(i):
        part = pl.ds(pl.multiple_of(i * chunk, chunk), chunk)
        slot = i % slots
        return pltpu.make_async_copy(trailing.at[part, columns], tiles.at[slot], sems.at[slot])

    fetched = fetch(index_ref[1], holder_ref, other_ref, panel, sem)
    load(0).start()
    fetched.wait()
    for i in range(1, slots):
        load(i).start()

    basis_ref[...] = dot_nt(panel[...], inverse_ref[...])
    high, low = split(basis_ref[...])
    both[:, :width] = high
    both[:, width:] = low
    copy = pltpu.make_async_copy(basis_ref, basis_out, sem)
    copy.start()

    @pl.loop(0, rows // chunk)
    def _(i):
        load(i).wait()
        part = pl.ds(pl.multiple_of(i * chunk, chunk), chunk)
        high, low = split(tiles[i % slots])
        right = both[...]
        value = dot_fast(high, right) + dot_fast(low, right)
        out_ref[part, :] = before_ref[part, :] + (value[:, :width] + value[:, width:])

        @pl.when(i + slots < count)
        def _():
            load(i + slots).start()

    copy.wait()


def product(index, trailing, inverse, before, holder, other):
    rows = trailing.shape[0]
    depth, width = holder.shape
    chunk = min(rows, 256)
    slots = min(4, rows // chunk)
    anywhere = pl.BlockSpec(memory_space=pl.ANY)
    near = pl.BlockSpec(memory_space=pltpu.VMEM)
    return pl.pallas_call(
        product_kernel,
        out_shape=(
            jax.ShapeDtypeStruct((rows, width), F32),
            jax.ShapeDtypeStruct((depth, width), F32),
        ),
        in_specs=[
            pl.BlockSpec(memory_space=pltpu.SMEM),
            anywhere,
            near,
            near,
            anywhere,
            anywhere,
        ],
        out_specs=(near, pl.BlockSpec(memory_space=pltpu.HBM)),
        scratch_shapes=[
            pltpu.VMEM((slots, chunk, depth), F32),
            pltpu.VMEM((depth, width), F32),
            pltpu.VMEM((depth, width), F32),
            pltpu.VMEM((depth, 2 * width), BF16),
            pltpu.SemaphoreType.DMA,
            pltpu.SemaphoreType.DMA((slots,)),
        ],
        compiler_params=pltpu.CompilerParams(vmem_limit_bytes=28 * 1024 * 1024),
        cost_estimate=pl.CostEstimate(
            flops=8 * rows * depth * width, bytes_accessed=4 * rows * depth, transcendentals=0
        ),
        name="product",
    )(index, trailing, inverse, before, holder, other)


def update_kernel(
    index_ref, trailing, left_ref, vectors_ref, holder_ref, other_ref, _,
    out, tiles, applied, right, sem, loads, stores,
):
    slots, chunk, depth = tiles.shape
    rows, width = left_ref.shape[0], vectors_ref.shape[1]
    count = rows // chunk
    ahead = max(slots - 2, 1)
    columns = pl.ds(pl.multiple_of(index_ref[0] * depth, depth), depth)

    def load(i):
        part = pl.ds(pl.multiple_of(i * chunk, chunk), chunk)
        slot = i % slots
        return pltpu.make_async_copy(trailing.at[part, columns], tiles.at[slot], loads.at[slot])

    def store(i):
        part = pl.ds(pl.multiple_of(i * chunk, chunk), chunk)
        slot = i % slots
        return pltpu.make_async_copy(tiles.at[slot], out.at[part, columns], stores.at[slot])

    fetched = fetch(index_ref[1], holder_ref, other_ref, applied, sem)
    for i in range(min(ahead, count)):
        load(i).start()

    fetched.wait()
    for place, ref in ((0, applied), (width, vectors_ref)):
        high, low = split(ref[...].T)
        right[place : place + width, :] = high
        right[2 * width + place : 3 * width + place, :] = low
        right[4 * width + place : 5 * width + place, :] = high

    @pl.loop(0, count)
    def _(i):
        @pl.when(i + ahead < count)
        def _():
            @pl.when(i + ahead >= slots)
            def _():
                store(i + ahead - slots).wait()

            load(i + ahead).start()

        load(i).wait()
        part = pl.ds(pl.multiple_of(i * chunk, chunk), chunk)
        high, low = split(left_ref[part, :])
        left = jnp.concatenate([high, high, low], axis=1)
        slot = i % slots
        tiles[slot] = tiles[slot] - dot_fast(left, right[...])
        store(i).start()

    for i in range(max(count - slots, 0), count):
        store(i).wait()


def update(index, trailing, left, vectors, holder, other, reduced):
    rows = trailing.shape[0]
    depth, width = vectors.shape
    chunk = min(rows, 256)
    slots = min(6, rows // chunk)
    anywhere = pl.BlockSpec(memory_space=pl.ANY)
    near = pl.BlockSpec(memory_space=pltpu.VMEM)
    aliases = {}
    if reduced is None:
        reduced = index
    else:
        aliases = {6: 0}
    return pl.pallas_call(
        update_kernel,
        out_shape=jax.ShapeDtypeStruct(trailing.shape, F32),
        in_specs=[
            pl.BlockSpec(memory_space=pltpu.SMEM),
            anywhere,
            near,
            near,
            anywhere,
            anywhere,
            anywhere,
        ],
        out_specs=anywhere,
        scratch_shapes=[
            pltpu.VMEM((slots, chunk, depth), F32),
            pltpu.VMEM((depth, width), F32),
            pltpu.VMEM((6 * width, depth), BF16),
            pltpu.SemaphoreType.DMA,
            pltpu.SemaphoreType.DMA((slots,)),
            pltpu.SemaphoreType.DMA((slots,)),
        ],
        input_output_aliases=aliases,
        compiler_params=pltpu.CompilerParams(vmem_limit_bytes=30 * 1024 * 1024),
        cost_estimate=pl.CostEstimate(
            flops=12 * rows * depth * width, bytes_accessed=8 * rows * depth, transcendentals=0
        ),
        name="update",
    )(index, trailing, left, vectors, holder, other, reduced)


def dot_three(a, b, dims):
    a_high, a_low = split(a)
    b_high, b_low = split(b)
    dot = lambda x, y: lax.dot_general(x, y, (dims, ((), ())), preferred_element_type=F32)
    return dot(a_high, b_high) + (dot(a_high, b_low) + dot(a_low, b_high))


def applied_kernel(
    index_ref, raw_ref, basis_ref, inverse_ref, lead_ref, give_ref, keep_ref, vectors_ref, inner_ref
):
    step = pl.program_id(0)
    half, width = raw_ref.shape
    value = dot_three(raw_ref[...], inverse_ref[...], ((1,), (1,)))
    value = value + jnp.where(index_ref[1] == 0, lead_ref[...], 0.0)
    first = index_ref[2] + (1 - (index_ref[0] ^ step)) * half
    rows = lax.broadcasted_iota(jnp.int32, (half, width), 0) + first
    lanes = lax.broadcasted_iota(jnp.int32, (half, width), 1)
    vectors = dot_three(basis_ref[...], inverse_ref[...], ((1,), (1,)))
    vectors = vectors + jnp.where(rows == lanes, 1.0, 0.0)
    vectors_ref[...] = vectors
    inner = dot_three(vectors, value, ((0,), (0,)))

    @pl.when(step == 0)
    def _():
        give_ref[...] = value
        inner_ref[...] = inner

    @pl.when(step == 1)
    def _():
        keep_ref[...] = value
        inner_ref[...] += inner


def applied_halves(index, raw, basis, inverse, trailing):
    rows, width = raw.shape
    half = rows // 2
    whole = pl.BlockSpec((half, width), lambda i, index: (0, 0))
    square = pl.BlockSpec((width, width), lambda i, index: (0, 0))
    piece = pl.BlockSpec((half, width), lambda i, index: (1 - (index[0] ^ i), 0))
    out = jax.ShapeDtypeStruct((half, width), F32)
    return pl.pallas_call(
        applied_kernel,
        out_shape=(
            out,
            out,
            jax.ShapeDtypeStruct((rows, width), F32),
            jax.ShapeDtypeStruct((width, width), F32),
        ),
        grid_spec=pltpu.PrefetchScalarGridSpec(
            num_scalar_prefetch=1,
            grid=(2,),
            in_specs=[piece, piece, square, piece],
            out_specs=(whole, whole, piece, square),
        ),
        compiler_params=pltpu.CompilerParams(vmem_limit_bytes=30 * 1024 * 1024),
        name="applied",
    )(index, raw, basis, inverse, trailing)


def after(value, *others):
    return lax.optimization_barrier((value, *others))[0]


def swap(value, axis, bit):
    count = lax.axis_size(axis)
    return lax.ppermute(value, axis, [(i, i ^ bit) for i in range(count)])


def bits_of(count):
    return [1 << b for b in range(count.bit_length() - 1)]


def sum_small(value, axis, bits):
    for bit in bits:
        value = value + swap(value, axis, bit)
    return value


class Gather:
    def __init__(self):
        self.row_n, self.col_n = lax.axis_size("row"), lax.axis_size("col")
        self.ratio = self.row_n // self.col_n
        self.away = (lax.axis_index("row") // self.ratio) ^ lax.axis_index("col")

    def move(self, value, holds, to_row):
        pairs = []
        for r in range(self.row_n):
            for c in range(self.col_n):
                if holds((r // self.ratio) ^ c):
                    pairs.append((r * self.col_n + c, to_row(r) * self.col_n + c))
        return lax.ppermute(value, ("row", "col"), pairs)

    def relay(self, value, done=0):
        for bit in reversed(bits_of(self.col_n)[1:]):
            if bit & done:
                continue
            moved = self.move(
                value, lambda d: d & ~done == 0, lambda r: r ^ (bit * self.ratio)
            )
            value = jnp.where((self.away & ~done) == bit, moved, value)
            done |= bit
        return value

    def second_half(self):
        return (self.away == self.col_n // 2).astype(jnp.int32)

    def relay_halves(self, value, piece, meanwhile):
        bit = self.col_n // 2
        first = self.move(piece, lambda d: d & ~bit == 0, lambda r: r ^ (bit * self.ratio))
        first, meanwhile = lax.optimization_barrier((first, meanwhile))
        pairs = []
        for r in range(self.row_n):
            c = r // self.ratio
            pairs.append((r * self.col_n + c, r * self.col_n + (c ^ bit)))
        second = lax.ppermute(first, ("row", "col"), pairs)
        moved = jnp.concatenate([first, second])
        return self.relay(jnp.where(self.away == bit, moved, value), bit), meanwhile

    def near(self, value):
        holds = lambda d: d & 1 == 0
        return (
            self.move(value, holds, lambda r: r ^ self.ratio),
            self.move(value, holds, lambda r: r ^ 1),
        )

    def across(self, moved_high):
        return self.move(moved_high, lambda d: d & 1 == 1, lambda r: r ^ 1)

    def rest(self, blocks):
        full = []
        for holder, other in blocks:
            full.append(jnp.where(self.away & 1 == 0, holder, other))
        for bit in bits_of(self.ratio)[1:]:
            full += [swap(value, "row", bit) for value in full]
        return [(value, value) for value in full[2:]]


def broadcast_col(value):
    col_n = lax.axis_size("col")
    col = lax.axis_index("col")
    for bit in bits_of(col_n):
        moved = lax.ppermute(value, "col", [(i, i + bit) for i in range(bit)])
        value = jnp.where((col >= bit) & (col < 2 * bit), moved, value)
    return value


def body(panel_block, trailing):
    shard_rows, width = panel_block.shape
    half = shard_rows // 2
    row, col = lax.axis_index("row"), lax.axis_index("col")
    row_bits, col_bits = bits_of(lax.axis_size("row")), bits_of(lax.axis_size("col"))
    gather = Gather()
    ratio = gather.ratio
    low = row % ratio
    lane = jnp.arange(width)

    def identity_rows(first):
        return ((first + jnp.arange(shard_rows))[:, None] == lane).astype(F32)

    def index_of(part):
        return jnp.stack([part ^ low, gather.away & 1]).astype(jnp.int32)

    gram = sum_small(dot_tn(panel_block, panel_block), "row", row_bits[:1])
    piece = lax.dynamic_slice_in_dim(panel_block, gather.second_half() * half, half, 0)
    relayed, gram = gather.relay_halves(panel_block, piece, gram)
    gram = sum_small(gram, "row", row_bits[1:])
    moved_high, moved_low = gather.near(after(relayed, gram))
    first_factor, first_inverse, first_basis, second = first_pass(gram, panel_block)

    second = sum_small(second, "row", row_bits[:1])
    moved_high, second = lax.optimization_barrier((moved_high, second))
    parts = [(relayed, moved_high), (moved_low, gather.across(moved_high))]
    raw, basis = product(
        index_of(0), trailing, first_inverse, jnp.zeros((shard_rows, width), F32), *parts[0]
    )
    bases = [basis]
    second = sum_small(second, "row", row_bits[:0:-1])
    parts += gather.rest(parts)
    for part in range(1, ratio):
        raw, basis = product(index_of(part), trailing, first_inverse, raw, *parts[part])
        bases.append(basis)
    second_upper, second_inverse = second_pass(second)

    mine = col & 1
    give, keep, vectors, inner = applied_halves(
        jnp.stack([mine, col, row * shard_rows]).astype(jnp.int32),
        raw,
        first_basis,
        second_inverse,
        trailing,
    )
    keep = keep + swap(give, "col", col_bits[0])
    inner = sum_small(inner, "row", row_bits)
    for bit in col_bits[1:]:
        moved, inner = lax.optimization_barrier((swap(keep, "col", bit), inner))
        keep = keep + moved
    keep = lax.optimization_barrier(keep)
    other = swap(keep, "col", col_bits[0])
    applied = jnp.zeros((shard_rows, width), F32)
    applied = lax.dynamic_update_slice_in_dim(applied, keep, mine * half, 0)
    applied = lax.dynamic_update_slice_in_dim(applied, other, (1 - mine) * half, 0)

    piece = jnp.where(mine == gather.second_half(), keep, other)
    top = sum(jnp.where(low == part, basis[:width], 0.0) for part, basis in enumerate(bases))
    top = broadcast_col(after(top, piece))
    band_block, kernel = small_pass(second_upper, second_inverse, first_factor, top)
    inner = sum_small(after(inner, piece), "col", col_bits)
    relayed, (inner, kernel) = gather.relay_halves(applied, piece, (inner, kernel))
    inner = dot_tn(kernel, dot_nn(inner, kernel))
    left = jnp.concatenate(
        [dot_nt(vectors, kernel), dot_nn(applied, kernel) - dot_nn(vectors, inner)], axis=1
    )
    block_vectors = [
        dot_nt(basis, second_inverse) + identity_rows((col * ratio + (part ^ low)) * shard_rows)
        for part, basis in enumerate(bases)
    ]
    relayed, left, *block_vectors = lax.optimization_barrier((relayed, left, *block_vectors))
    moved_high, moved_low = gather.near(relayed)
    parts = [(relayed, moved_high), (moved_low, gather.across(moved_high))]
    reduced = update(index_of(0), trailing, left, block_vectors[0], *parts[0], None)
    parts += gather.rest(parts)
    for part in range(1, ratio):
        reduced = update(index_of(part), trailing, left, block_vectors[part], *parts[part], reduced)
    return (reduced, band_block, first_factor)


def solution(mesh):
    in_specs = (P("row", None), P("row", "col"))
    out_specs = (P("row", "col"), P(), P())
    return jax.shard_map(body, mesh=mesh, in_specs=in_specs, out_specs=out_specs, check_vma=False)
```

```python
import functools

import jax
import jax.numpy as jnp
from jax import lax
from jax.experimental import pallas as pl
from jax.experimental.pallas import tpu as pltpu
from jax.sharding import PartitionSpec as P

HIGH = lax.Precision.HIGHEST
F32 = jnp.float32
BF16 = jnp.bfloat16
SUB = 8


def dot_nn(a, b):
    return lax.dot_general(a, b, (((1,), (0,)), ((), ())), precision=HIGH, preferred_element_type=F32)


def dot_nt(a, b):
    return lax.dot_general(a, b, (((1,), (1,)), ((), ())), precision=HIGH, preferred_element_type=F32)


def dot_tn(a, b):
    return lax.dot_general(a, b, (((0,), (0,)), ((), ())), precision=HIGH, preferred_element_type=F32)


def dot_fast(a, b):
    return lax.dot_general(a, b, (((1,), (0,)), ((), ())), preferred_element_type=F32)


def lane_copy(tile, lane):
    return jnp.broadcast_to(tile[:, lane : lane + 1], tile.shape)


def row_copy(tile, row):
    return jnp.broadcast_to(tile[row : row + 1, :], tile.shape)


def cholesky_tiles(tiles):
    size = tiles[0].shape[1]
    count = len(tiles)
    tiles = list(tiles)
    lanes = lax.broadcasted_iota(jnp.int32, (SUB, size), 1)
    subs = lax.broadcasted_iota(jnp.int32, (SUB, size), 0)
    upper, inverse = [], []
    for block in range(count):
        base = block * SUB
        here = (lanes >= base) & (lanes < base + SUB)
        columns = [[lane_copy(tiles[i], base + k) for k in range(SUB)] for i in range(block, count)]
        right = jnp.where(lanes >= base, tiles[block], 0.0)
        left = jnp.where(lanes < base, tiles[block], 0.0)
        left = jnp.where(lanes - base == subs, 1.0, left)
        out_upper, out_inverse = jnp.zeros_like(right), jnp.zeros_like(left)
        below = [jnp.where(here, 0.0, tiles[i]) for i in range(block + 1, count)]
        for k in range(SUB):
            diag = columns[0]
            pivot = row_copy(diag[k], k)
            root = lax.rsqrt(pivot)
            recip = 1.0 / pivot
            right_row, left_row = row_copy(right, k), row_copy(left, k)
            out_upper = jnp.where(subs == k, right_row * root, out_upper)
            out_inverse = jnp.where(subs == k, left_row * root, out_inverse)
            packed = jnp.where(lanes < base + SUB, left_row, right_row) * recip
            rows = {l: row_copy(diag[l], k) * recip for l in range(k + 1, SUB)}
            factor = jnp.where(subs > k, diag[k], 0.0)
            right = right - factor * (right_row * recip)
            left = left - factor * (left_row * recip)
            for i in range(count - block):
                for l in range(k + 1, SUB):
                    if i == 0:
                        columns[0][l] = columns[0][l] - factor * rows[l]
                    else:
                        columns[i][l] = columns[i][l] - columns[i][k] * rows[l]
                if i:
                    below[i - 1] = below[i - 1] - columns[i][k] * packed
        for i in range(block + 1, count):
            tiles[i] = below[i - block - 1]
        upper.append(jnp.where(lanes >= base + subs, out_upper, 0.0))
        inverse.append(out_inverse)
    return upper, inverse


def invert_tiles(tiles):
    size = tiles[0].shape[1]
    count = len(tiles)
    tiles = list(tiles)
    lanes = lax.broadcasted_iota(jnp.int32, (SUB, size), 1)
    subs = lax.broadcasted_iota(jnp.int32, (SUB, size), 0)
    for block in range(count):
        base = block * SUB
        here = (lanes >= base) & (lanes < base + SUB)
        columns = [[lane_copy(tiles[i], base + k) for k in range(SUB)] for i in range(count)]
        diag = list(columns[block])
        row = jnp.where(here, jnp.where(lanes - base == subs, 1.0, 0.0), tiles[block])
        for k in range(SUB):
            recip = 1.0 / row_copy(diag[k], k)
            own = subs == k
            pivot_row = row_copy(row, k) * recip
            rows = {l: row_copy(diag[l], k) * recip for l in range(k + 1, SUB)}
            row = jnp.where(own, pivot_row, row - diag[k] * pivot_row)
            for l in range(k + 1, SUB):
                diag[l] = jnp.where(own, rows[l], diag[l] - diag[k] * rows[l])
        spread = [row_copy(row, k) for k in range(SUB)]
        for i in range(count):
            if i == block:
                continue
            value = jnp.where(here, 0.0, tiles[i])
            for k in range(SUB):
                value = value - columns[i][k] * spread[k]
            tiles[i] = value
        tiles[block] = row
    return tiles


def tiles_of(ref):
    return [ref[i * SUB : (i + 1) * SUB, :] for i in range(ref.shape[0] // SUB)]


def split(value):
    high = value.astype(BF16)
    return high, (value - high.astype(F32)).astype(BF16)


def first_kernel(
    gram_ref, panel, factor_ref, inverse_ref, basis_out, second_ref, panel_ref, basis_ref, sem
):
    fetched = pltpu.make_async_copy(panel, panel_ref, sem.at[0])
    fetched.start()
    upper, inverse = cholesky_tiles(tiles_of(gram_ref))
    inverse_ref[...] = jnp.concatenate(inverse, axis=0)
    fetched.wait()
    basis_ref[...] = dot_nt(panel_ref[...], inverse_ref[...])
    copy = pltpu.make_async_copy(basis_ref, basis_out, sem.at[1])
    copy.start()
    factor_ref[...] = jnp.concatenate(upper, axis=0).T
    high, low = split(basis_ref[...])
    width = low.shape[1]
    value = lax.dot_general(
        high,
        jnp.concatenate([high, low], axis=1),
        (((0,), (0,)), ((), ())),
        preferred_element_type=F32,
    )
    cross = value[:, width:]
    second_ref[...] = value[:, :width] + (cross + cross.T)
    copy.wait()


def first_pass(gram, panel):
    square = jax.ShapeDtypeStruct(gram.shape, F32)
    near = pl.BlockSpec(memory_space=pltpu.VMEM)
    return pl.pallas_call(
        first_kernel,
        out_shape=(square, square, jax.ShapeDtypeStruct(panel.shape, F32), square),
        in_specs=[near, pl.BlockSpec(memory_space=pl.ANY)],
        out_specs=(near, near, pl.BlockSpec(memory_space=pltpu.HBM), near),
        scratch_shapes=[
            pltpu.VMEM(panel.shape, F32),
            pltpu.VMEM(panel.shape, F32),
            pltpu.SemaphoreType.DMA((2,)),
        ],
        compiler_params=pltpu.CompilerParams(vmem_limit_bytes=24 * 1024 * 1024),
        name="first_pass",
    )(gram, panel)


def second_kernel(gram_ref, upper_ref, inverse_ref):
    upper, inverse = cholesky_tiles(tiles_of(gram_ref))
    upper_ref[...] = jnp.concatenate(upper, axis=0)
    inverse_ref[...] = jnp.concatenate(inverse, axis=0)


def second_pass(gram):
    square = jax.ShapeDtypeStruct(gram.shape, F32)
    return pl.pallas_call(
        second_kernel,
        out_shape=(square, square),
        compiler_params=pltpu.CompilerParams(vmem_limit_bytes=8 * 1024 * 1024),
        name="second_pass",
    )(gram)


def small_kernel(upper_ref, inverse_ref, first_ref, top_ref, band_ref, kernel_ref):
    band_ref[...] = -dot_nt(upper_ref[...], first_ref[...])
    size = upper_ref.shape[0]
    rows = lax.broadcasted_iota(jnp.int32, (size, size), 0)
    lanes = lax.broadcasted_iota(jnp.int32, (size, size), 1)
    eye = jnp.where(rows == lanes, 1.0, 0.0)
    kernel_ref[...] = eye + dot_nt(inverse_ref[...], top_ref[...])
    kernel_ref[...] = jnp.concatenate(invert_tiles(tiles_of(kernel_ref)), axis=0)


def small_pass(upper, inverse, first_factor, top):
    square = jax.ShapeDtypeStruct(upper.shape, F32)
    return pl.pallas_call(
        small_kernel,
        out_shape=(square, square),
        compiler_params=pltpu.CompilerParams(vmem_limit_bytes=8 * 1024 * 1024),
        name="small_pass",
    )(upper, inverse, first_factor, top)


def fetch(away, holder, other, into, sem):
    @pl.when(away == 0)
    def _():
        pltpu.make_async_copy(holder, into, sem).start()

    @pl.when(away != 0)
    def _():
        pltpu.make_async_copy(other, into, sem).start()

    return pltpu.make_async_copy(holder, into, sem)


def product_kernel(
    index_ref, trailing, inverse_ref, before_ref, holder_ref, other_ref,
    out_ref, basis_out, tiles, panel, basis_ref, both, sem, sems,
):
    slots, chunk, depth = tiles.shape
    rows, width = out_ref.shape
    count = rows // chunk
    columns = pl.ds(pl.multiple_of(index_ref[0] * depth, depth), depth)

    def load(i):
        part = pl.ds(pl.multiple_of(i * chunk, chunk), chunk)
        slot = i % slots
        return pltpu.make_async_copy(trailing.at[part, columns], tiles.at[slot], sems.at[slot])

    fetched = fetch(index_ref[1], holder_ref, other_ref, panel, sem)
    load(0).start()
    fetched.wait()
    for i in range(1, slots):
        load(i).start()

    basis_ref[...] = dot_nt(panel[...], inverse_ref[...])
    high, low = split(basis_ref[...])
    both[:, :width] = high
    both[:, width:] = low
    copy = pltpu.make_async_copy(basis_ref, basis_out, sem)
    copy.start()

    @pl.loop(0, rows // chunk)
    def _(i):
        load(i).wait()
        part = pl.ds(pl.multiple_of(i * chunk, chunk), chunk)
        high, low = split(tiles[i % slots])
        right = both[...]
        value = dot_fast(high, right) + dot_fast(low, right)
        out_ref[part, :] = before_ref[part, :] + (value[:, :width] + value[:, width:])

        @pl.when(i + slots < count)
        def _():
            load(i + slots).start()

    copy.wait()


def product(index, trailing, inverse, before, holder, other):
    rows = trailing.shape[0]
    depth, width = holder.shape
    chunk = min(rows, 256)
    slots = min(4, rows // chunk)
    anywhere = pl.BlockSpec(memory_space=pl.ANY)
    near = pl.BlockSpec(memory_space=pltpu.VMEM)
    return pl.pallas_call(
        product_kernel,
        out_shape=(
            jax.ShapeDtypeStruct((rows, width), F32),
            jax.ShapeDtypeStruct((depth, width), F32),
        ),
        in_specs=[
            pl.BlockSpec(memory_space=pltpu.SMEM),
            anywhere,
            near,
            near,
            anywhere,
            anywhere,
        ],
        out_specs=(near, pl.BlockSpec(memory_space=pltpu.HBM)),
        scratch_shapes=[
            pltpu.VMEM((slots, chunk, depth), F32),
            pltpu.VMEM((depth, width), F32),
            pltpu.VMEM((depth, width), F32),
            pltpu.VMEM((depth, 2 * width), BF16),
            pltpu.SemaphoreType.DMA,
            pltpu.SemaphoreType.DMA((slots,)),
        ],
        compiler_params=pltpu.CompilerParams(vmem_limit_bytes=28 * 1024 * 1024),
        cost_estimate=pl.CostEstimate(
            flops=8 * rows * depth * width, bytes_accessed=4 * rows * depth, transcendentals=0
        ),
        name="product",
    )(index, trailing, inverse, before, holder, other)


def update_kernel(count_left, has_vectors, has_applied, index_ref, source, *refs):
    lefts, refs = refs[:count_left], list(refs[count_left:])
    vectors_ref = refs.pop(0) if has_vectors else None
    holder_ref, other_ref = (refs.pop(0), refs.pop(0)) if has_applied else (None, None)
    _, out, tiles, right, applied, sem, loads, stores = refs
    slots, chunk, depth = tiles.shape
    rows, width = lefts[0].shape
    count = rows // chunk
    ahead = max(slots - 2, 1)
    columns = pl.ds(pl.multiple_of(index_ref[0] * depth, depth), depth)

    def place(array, i):
        part = pl.ds(pl.multiple_of(i * chunk, chunk), chunk)
        return array.at[part, columns] if array.shape[1] > depth else array.at[part]

    def load(i):
        slot = i % slots
        return pltpu.make_async_copy(place(source, i), tiles.at[slot], loads.at[slot])

    def store(i):
        slot = i % slots
        return pltpu.make_async_copy(tiles.at[slot], place(out, i), stores.at[slot])

    if has_applied:
        fetched = fetch(index_ref[1], holder_ref, other_ref, applied, sem)
    for i in range(min(ahead, count)):
        load(i).start()

    pieces = []
    if has_applied:
        fetched.wait()
        pieces.append(applied)
    if has_vectors:
        pieces.append(vectors_ref)
    for n, ref in enumerate(pieces):
        high, low = split(ref[...].T)
        for term, value in enumerate((high, low, high)):
            start = (term * count_left + n) * width
            right[start : start + width, :] = value

    @pl.loop(0, count)
    def _(i):
        @pl.when(i + ahead < count)
        def _():
            @pl.when(i + ahead >= slots)
            def _():
                store(i + ahead - slots).wait()

            load(i + ahead).start()

        load(i).wait()
        part = pl.ds(pl.multiple_of(i * chunk, chunk), chunk)
        terms = [split(ref[part, :]) for ref in lefts]
        high, low = [value for value, _ in terms], [value for _, value in terms]
        left = jnp.concatenate(high + high + low, axis=1)
        slot = i % slots
        tiles[slot] = tiles[slot] - dot_fast(left, right[...])
        store(i).start()

    for i in range(max(count - slots, 0), count):
        store(i).wait()


def update(index, source, lefts, vectors, applied, reduced, out_columns):
    rows, width = lefts[0].shape
    depth = (applied[0] if vectors is None else vectors).shape[0]
    chunk = min(rows, 256)
    slots = min(6, rows // chunk)
    anywhere = pl.BlockSpec(memory_space=pl.ANY)
    near = pl.BlockSpec(memory_space=pltpu.VMEM)
    operands = [index, source, *lefts]
    specs = [pl.BlockSpec(memory_space=pltpu.SMEM), anywhere, *[near for _ in lefts]]
    if vectors is not None:
        operands.append(vectors)
        specs.append(near)
    if applied is not None:
        operands += applied
        specs += [anywhere, anywhere]
    aliases = {} if reduced is None else {len(operands): 0}
    operands.append(index if reduced is None else reduced)
    specs.append(anywhere)
    return pl.pallas_call(
        functools.partial(update_kernel, len(lefts), vectors is not None, applied is not None),
        out_shape=jax.ShapeDtypeStruct((rows, out_columns), F32),
        in_specs=specs,
        out_specs=anywhere,
        scratch_shapes=[
            pltpu.VMEM((slots, chunk, depth), F32),
            pltpu.VMEM((3 * len(lefts) * width, depth), BF16),
            pltpu.VMEM((depth, width), F32),
            pltpu.SemaphoreType.DMA,
            pltpu.SemaphoreType.DMA((slots,)),
            pltpu.SemaphoreType.DMA((slots,)),
        ],
        input_output_aliases=aliases,
        compiler_params=pltpu.CompilerParams(vmem_limit_bytes=24 * 1024 * 1024),
        cost_estimate=pl.CostEstimate(
            flops=6 * len(lefts) * rows * depth * width,
            bytes_accessed=8 * rows * depth,
            transcendentals=0,
        ),
        name="update",
    )(*operands)


def dot_three(a, b, dims):
    a_high, a_low = split(a)
    b_high, b_low = split(b)
    dot = lambda x, y: lax.dot_general(x, y, (dims, ((), ())), preferred_element_type=F32)
    return dot(a_high, b_high) + (dot(a_high, b_low) + dot(a_low, b_high))


def applied_kernel(
    index_ref, raw_ref, basis_ref, inverse_ref, lead_ref, give_ref, keep_ref, vectors_ref, inner_ref
):
    step = pl.program_id(0)
    half, width = raw_ref.shape
    value = dot_three(raw_ref[...], inverse_ref[...], ((1,), (1,)))
    value = value + jnp.where(index_ref[1] == 0, lead_ref[...], 0.0)
    first = index_ref[2] + (1 - (index_ref[0] ^ step)) * half
    rows = lax.broadcasted_iota(jnp.int32, (half, width), 0) + first
    lanes = lax.broadcasted_iota(jnp.int32, (half, width), 1)
    vectors = dot_three(basis_ref[...], inverse_ref[...], ((1,), (1,)))
    vectors = vectors + jnp.where(rows == lanes, 1.0, 0.0)
    vectors_ref[...] = vectors
    inner = dot_three(vectors, value, ((0,), (0,)))

    @pl.when(step == 0)
    def _():
        give_ref[...] = value
        inner_ref[...] = inner

    @pl.when(step == 1)
    def _():
        keep_ref[...] = value
        inner_ref[...] += inner


def applied_halves(index, raw, basis, inverse, trailing):
    rows, width = raw.shape
    half = rows // 2
    whole = pl.BlockSpec((half, width), lambda i, index: (0, 0))
    square = pl.BlockSpec((width, width), lambda i, index: (0, 0))
    piece = pl.BlockSpec((half, width), lambda i, index: (1 - (index[0] ^ i), 0))
    out = jax.ShapeDtypeStruct((half, width), F32)
    return pl.pallas_call(
        applied_kernel,
        out_shape=(
            out,
            out,
            jax.ShapeDtypeStruct((rows, width), F32),
            jax.ShapeDtypeStruct((width, width), F32),
        ),
        grid_spec=pltpu.PrefetchScalarGridSpec(
            num_scalar_prefetch=1,
            grid=(2,),
            in_specs=[piece, piece, square, piece],
            out_specs=(whole, whole, piece, square),
        ),
        compiler_params=pltpu.CompilerParams(vmem_limit_bytes=30 * 1024 * 1024),
        name="applied",
    )(index, raw, basis, inverse, trailing)


def after(value, *others):
    return lax.optimization_barrier((value, *others))[0]


def swap(value, axis, bit):
    count = lax.axis_size(axis)
    return lax.ppermute(value, axis, [(i, i ^ bit) for i in range(count)])


def bits_of(count):
    return [1 << b for b in range(count.bit_length() - 1)]


def sum_small(value, axis, bits):
    for bit in bits:
        value = value + swap(value, axis, bit)
    return value


class Gather:
    def __init__(self):
        self.row_n, self.col_n = lax.axis_size("row"), lax.axis_size("col")
        self.ratio = self.row_n // self.col_n
        self.away = (lax.axis_index("row") // self.ratio) ^ lax.axis_index("col")

    def move(self, value, holds, to_row):
        pairs = []
        for r in range(self.row_n):
            for c in range(self.col_n):
                if holds((r // self.ratio) ^ c):
                    pairs.append((r * self.col_n + c, to_row(r) * self.col_n + c))
        return lax.ppermute(value, ("row", "col"), pairs)

    def relay(self, value, done=0):
        for bit in reversed(bits_of(self.col_n)[1:]):
            if bit & done:
                continue
            moved = self.move(
                value, lambda d: d & ~done == 0, lambda r: r ^ (bit * self.ratio)
            )
            value = jnp.where((self.away & ~done) == bit, moved, value)
            done |= bit
        return value

    def second_half(self):
        return (self.away == self.col_n // 2).astype(jnp.int32)

    def relay_halves(self, value, piece, meanwhile):
        bit = self.col_n // 2
        first = self.move(piece, lambda d: d & ~bit == 0, lambda r: r ^ (bit * self.ratio))
        first, meanwhile = lax.optimization_barrier((first, meanwhile))
        pairs = []
        for r in range(self.row_n):
            c = r // self.ratio
            pairs.append((r * self.col_n + c, r * self.col_n + (c ^ bit)))
        second = lax.ppermute(first, ("row", "col"), pairs)
        moved = jnp.concatenate([first, second])
        return self.relay(jnp.where(self.away == bit, moved, value), bit), meanwhile

    def near(self, value):
        holds = lambda d: d & 1 == 0
        return (
            self.move(value, holds, lambda r: r ^ self.ratio),
            self.move(value, holds, lambda r: r ^ 1),
        )

    def across(self, moved_high):
        return self.move(moved_high, lambda d: d & 1 == 1, lambda r: r ^ 1)

    def rest(self, blocks):
        full = []
        for holder, other in blocks:
            full.append(jnp.where(self.away & 1 == 0, holder, other))
        for bit in bits_of(self.ratio)[1:]:
            full += [swap(value, "row", bit) for value in full]
        return [(value, value) for value in full[2:]]


def broadcast_col(value):
    col_n = lax.axis_size("col")
    col = lax.axis_index("col")
    for bit in bits_of(col_n):
        moved = lax.ppermute(value, "col", [(i, i + bit) for i in range(bit)])
        value = jnp.where((col >= bit) & (col < 2 * bit), moved, value)
    return value


def body(panel_block, trailing):
    shard_rows, width = panel_block.shape
    half = shard_rows // 2
    row, col = lax.axis_index("row"), lax.axis_index("col")
    row_bits, col_bits = bits_of(lax.axis_size("row")), bits_of(lax.axis_size("col"))
    gather = Gather()
    ratio = gather.ratio
    low = row % ratio
    lane = jnp.arange(width)

    def identity_rows(first):
        return ((first + jnp.arange(shard_rows))[:, None] == lane).astype(F32)

    def index_of(part):
        return jnp.stack([part ^ low, gather.away & 1]).astype(jnp.int32)

    gram = sum_small(dot_tn(panel_block, panel_block), "row", row_bits[:1])
    piece = lax.dynamic_slice_in_dim(panel_block, gather.second_half() * half, half, 0)
    relayed, gram = gather.relay_halves(panel_block, piece, gram)
    gram = sum_small(gram, "row", row_bits[1:])
    moved_high, moved_low = gather.near(after(relayed, gram))
    first_factor, first_inverse, first_basis, second = first_pass(gram, panel_block)

    second = sum_small(second, "row", row_bits[:1])
    moved_high, second = lax.optimization_barrier((moved_high, second))
    parts = [(relayed, moved_high), (moved_low, gather.across(moved_high))]
    raw, basis = product(
        index_of(0), trailing, first_inverse, jnp.zeros((shard_rows, width), F32), *parts[0]
    )
    bases = [basis]
    second = sum_small(second, "row", row_bits[:0:-1])
    parts += gather.rest(parts)
    for part in range(1, ratio):
        raw, basis = product(index_of(part), trailing, first_inverse, raw, *parts[part])
        bases.append(basis)
    second_upper, second_inverse = second_pass(second)

    mine = col & 1
    give, keep, vectors, inner = applied_halves(
        jnp.stack([mine, col, row * shard_rows]).astype(jnp.int32),
        raw,
        first_basis,
        second_inverse,
        trailing,
    )
    keep = keep + swap(give, "col", col_bits[0])
    inner = sum_small(inner, "row", row_bits)
    for bit in col_bits[1:]:
        moved, inner = lax.optimization_barrier((swap(keep, "col", bit), inner))
        keep = keep + moved
    keep = lax.optimization_barrier(keep)
    other = swap(keep, "col", col_bits[0])
    applied = jnp.zeros((shard_rows, width), F32)
    applied = lax.dynamic_update_slice_in_dim(applied, keep, mine * half, 0)
    applied = lax.dynamic_update_slice_in_dim(applied, other, (1 - mine) * half, 0)

    piece = jnp.where(mine == gather.second_half(), keep, other)
    top = sum(jnp.where(low == part, basis[:width], 0.0) for part, basis in enumerate(bases))
    top = broadcast_col(after(top, piece))
    band_block, kernel = small_pass(second_upper, second_inverse, first_factor, top)
    inner = sum_small(after(inner, piece), "col", col_bits)
    relayed, (inner, kernel) = gather.relay_halves(applied, piece, (inner, kernel))
    inner = dot_tn(kernel, dot_nn(inner, kernel))
    lefts = [dot_nt(vectors, kernel), dot_nn(applied, kernel) - dot_nn(vectors, inner)]
    block_vectors = [
        dot_nt(after(basis, kernel), second_inverse)
        + identity_rows((col * ratio + (part ^ low)) * shard_rows)
        for part, basis in enumerate(bases)
    ]
    relayed, *lefts = lax.optimization_barrier((relayed, *lefts, *block_vectors))
    lefts, block_vectors = lefts[:2], lefts[2:]
    moved_high, moved_low = gather.near(relayed)
    columns = trailing.shape[1]

    last = ratio - 1
    started = update(
        index_of(last), trailing, lefts[1:], block_vectors[last], None, None, shard_rows
    )
    moved_high, started = lax.optimization_barrier((moved_high, started))
    parts = [(relayed, moved_high), (moved_low, gather.across(moved_high))]
    parts += gather.rest(parts)
    reduced = None
    for part in range(last):
        reduced = update(
            index_of(part), trailing, lefts, block_vectors[part], parts[part], reduced, columns
        )
    reduced = update(index_of(last), started, lefts[:1], None, parts[last], reduced, columns)
    return (reduced, band_block, first_factor)


def solution(mesh):
    in_specs = (P("row", None), P("row", "col"))
    out_specs = (P("row", "col"), P(), P())
    return jax.shard_map(body, mesh=mesh, in_specs=in_specs, out_specs=out_specs, check_vma=False)
```
